128 devices in a mesh: lat: 8 (over z_lo, y), lon: 16 (over z_hi, x, core).
Axes of the slice: x: 4, y: 4, z: 4 (z_hi: 2, z_lo: 2; z = z_hi * 2 + z_lo), core: 2. Of those that a mesh axis runs over, the one named last changes fastest.
Arguments:
- tokens: bfloat16 [8, 96, 36864], P(None, 'lat', 'lon'), may hold values from -6 to 6
- surface_ids: int32 [96, 192], P('lat', 'lon'), may hold values from 0 to 2
- surface_embed: bfloat16 [3, 192], replicated, may hold values from -5 to 5
- type_index: int32 [16], P('lat'), may hold values from 0 to 15
- bias_plain: bfloat16 [1271808], P('lon'), may hold values from -4 to 300
- bias_shift: bfloat16 [1271808], P('lon'), may hold values from -4 to 300
- w_qkv: bfloat16 [2, 110592], replicated, may hold values from -0.21875 to 0.21875
- w_proj: bfloat16 [2, 36864], replicated, may hold values from -0.875 to 0.875
- w_up: bfloat16 [2, 192, 768], replicated, may hold values from -0.4375 to 0.4375
- w_down: bfloat16 [2, 147456], replicated, may hold values from -0.21875 to 0.21875
Outputs:
- evolved: bfloat16 [8, 96, 36864], P(None, 'lat', 'lon')
The draws below stay inside these ranges and needn't reach their ends.
All inputs are finite; a program needn't handle non-finite values.
Results may differ from the reference program's by a relative error of at most 0.015.
Values may be sent and summed in bfloat16 or wider, within the bound.
A program may use at most 128 MiB of HBM per device.

```python
import jax
import jax.numpy as jnp
from jax import lax

HEADS = 6
HEAD_DIM = 32
C = 192
Z = 8
WZ = 2
WH = 6
WW = 12
NH = 96
NW = 192
LEVWIN = 4
TYPES_LAT = 16
RELPOS = 3312


def flatten_table(table):
    return table.transpose(0, 2, 3, 1).reshape(-1)


def draw_bias_plain(key, part):
    key = jax.random.fold_in(key, 11)
    shape = (LEVWIN, TYPES_LAT, HEADS, RELPOS)
    base_key = jax.random.fold_in(key, 0)
    return flatten_table(jnp.clip(jax.random.normal(base_key, shape, jnp.float32), -4.0, 4.0)).astype(jnp.bfloat16)


def draw_bias_shift(key, part):
    key = jax.random.fold_in(key, 12)
    shape = (LEVWIN, TYPES_LAT, HEADS, RELPOS)
    base_key = jax.random.fold_in(key, 0)
    return flatten_table(jnp.clip(jax.random.normal(base_key, shape, jnp.float32), -4.0, 4.0)).astype(jnp.bfloat16)


def place_ends(values, rng, smallest, high):
    longest = values.shape.index(max(values.shape))
    spots = []
    for shift in (0, 1):
        where = [jax.random.randint(jax.random.fold_in(rng, axis), (), 0, length) for axis, length in enumerate(values.shape)]
        where[longest] = (where[longest] + shift) % values.shape[longest]
        spots.append(tuple(where))
    return values.at[spots[0]].set(smallest).at[spots[1]].set(high)


def steps_of(rng, extent, cuts, low, largest):
    level, own = 1.0, jax.random.fold_in(rng, 6)
    for position, shards_of in cuts:
        heights = jnp.exp(jax.random.uniform(jax.random.fold_in(own, position), (shards_of,), jnp.float32, low / len(cuts), largest / len(cuts)))
        level = level * jnp.repeat(heights, extent[position] // shards_of).reshape([-1 if axis == position else 1 for axis in range(len(extent))])
    return level


def normal_values(key, extent, scale, limit, pieces=(), kind=jnp.bfloat16):
    result = scale * jax.random.normal(key, extent, jnp.float32)
    if pieces:
        result = result * steps_of(key, extent, pieces, -0.22, 0.18)
    return jnp.clip(result, -limit, limit).astype(kind)


def setup_inputs(seed: int = 0) -> dict:
    keys = jax.random.split(jax.random.key(seed), 11)
    return {
        "tokens": normal_values(keys[0], (Z, NH, NW * C), 1.0, 6.0, ((1, 8), (2, 16))),
        "surface_ids": place_ends(jax.random.randint(keys[1], (NH, NW), 0, 3), jax.random.fold_in(keys[1], 1), 0, 2).astype(jnp.int32),
        "surface_embed": normal_values(keys[2], (3, C), 1.0, 5.0),
        "type_index": place_ends(jax.random.randint(keys[3], (TYPES_LAT,), 0, TYPES_LAT), jax.random.fold_in(keys[3], 1), 0, TYPES_LAT - 1).astype(jnp.int32),
        "bias_plain": draw_bias_plain(jax.random.fold_in(keys[10], 71), 0),
        "bias_shift": draw_bias_shift(jax.random.fold_in(keys[10], 71), 0),
        "w_qkv": normal_values(keys[6], (2, 3 * C * C), (4 * C) ** -0.5, 0.21875),
        "w_proj": normal_values(keys[7], (2, C * C), (C // 4) ** -0.5, 0.875),
        "w_up": normal_values(keys[8], (2, C, 4 * C), C ** -0.5, 0.4375),
        "w_down": normal_values(keys[9], (2, 4 * C * C), (4 * C) ** -0.5, 0.21875),
    }


def layer_norm(stream):
    values = stream.astype(jnp.float32)
    center = lax.optimization_barrier(jnp.mean(values, axis=-1, keepdims=True))
    spread = lax.optimization_barrier(jnp.mean(jnp.square(values - center), axis=-1, keepdims=True))
    return (values - center) * lax.rsqrt(spread + 1e-05)

def position_index():
    token_slot = jnp.arange(WZ * WH * WW, dtype=jnp.int32)
    level_pos = token_slot // (WH * WW)
    lat_pos = token_slot // WW % WH
    lon_pos = token_slot % WW
    index = (level_pos[:, None] * WZ + level_pos[None, :]) * WH + lat_pos[:, None]
    index = (index * WH + lat_pos[None, :]) * (2 * WW - 1)
    return index + lon_pos[:, None] - lon_pos[None, :] + WW - 1

def group_labels(levels, rows, total_rows, band_start):
    token_slot = jnp.arange(WZ * WH * WW, dtype=jnp.int32)
    level_index = jnp.arange(levels // WZ, dtype=jnp.int32)[:, None, None] * WZ + (token_slot // (WH * WW))[None, None, :]
    lat_index = band_start + jnp.arange(rows // WH, dtype=jnp.int32)[None, :, None] * WH + (token_slot // WW % WH)[None, None, :]
    level_group = (level_index >= levels - WZ).astype(jnp.int32) + (level_index >= levels - WZ // 2).astype(jnp.int32)
    lat_group = (lat_index >= total_rows - WH).astype(jnp.int32) + (lat_index >= total_rows - WH // 2).astype(jnp.int32)
    return level_group * 3 + lat_group

def to_windows(stream):
    levels, rows, columns, width = stream.shape
    shaped = stream.reshape(levels // WZ, WZ, rows // WH, WH, columns // WW, WW, width)
    shaped = shaped.transpose(0, 2, 4, 1, 3, 5, 6)
    return shaped.reshape(levels // WZ, rows // WH, columns // WW, WZ * WH * WW, width)

def from_windows(windowed, levels, rows, columns):
    width = windowed.shape[-1]
    shaped = windowed.reshape(levels // WZ, rows // WH, columns // WW, WZ, WH, WW, width)
    return shaped.transpose(0, 3, 1, 4, 2, 5, 6).reshape(levels, rows, columns, width)

def attend_windows(packed, table_rows, labels, positions):
    width = packed.shape[-1] // 3
    head_size = width // HEADS
    shape = packed.shape[:-1] + (HEADS, head_size)
    queries = packed[..., :width].astype(jnp.float32).reshape(shape)
    keys_part = packed[..., width:2 * width].astype(jnp.float32).reshape(shape)
    values_part = packed[..., 2 * width:].astype(jnp.float32).reshape(shape)
    scores = jnp.einsum('wqhd,wkhd->whqk', queries, keys_part) * head_size ** (-0.5)
    scores = scores + table_rows.astype(jnp.float32)[:, positions][None]
    same_group = labels[:, None] == labels[None, :]
    scores = jnp.where(same_group[None, None], scores, -jnp.inf)
    attention_weights = jax.nn.softmax(scores, axis=-1).astype(jnp.bfloat16)
    attention_weights = lax.optimization_barrier(attention_weights).astype(jnp.float32)
    mixed = jnp.einsum('whqk,wkhd->wqhd', attention_weights, values_part)
    return mixed.astype(jnp.bfloat16).reshape(packed.shape[:-1] + (width,))

def run_block(stream, w_qkv, w_proj, w_up, w_down, table, type_index, labels):
    levels, rows, columns, width = stream.shape
    normed = layer_norm(stream).astype(jnp.bfloat16)
    packed = jnp.dot(normed.reshape(-1, width), w_qkv, preferred_element_type=jnp.float32).astype(jnp.bfloat16)
    windowed = to_windows(packed.reshape(levels, rows, columns, 3 * width))
    level_windows, lat_windows = (windowed.shape[0], windowed.shape[1])
    flat = windowed.reshape((level_windows * lat_windows,) + windowed.shape[2:])
    flat_labels = labels.reshape(level_windows * lat_windows, -1)
    positions = position_index()

    def per_item(item_index):
        level_window = item_index // lat_windows
        lat_window = item_index % lat_windows
        table_rows = table[level_window, type_index[lat_window]]
        return attend_windows(flat[item_index], table_rows, flat_labels[item_index], positions)
    attended = lax.map(per_item, jnp.arange(level_windows * lat_windows, dtype=jnp.int32))
    attended = attended.reshape(windowed.shape[:-1] + (width,))
    attended = from_windows(attended, levels, rows, columns)
    projected = jnp.dot(attended.reshape(-1, width), w_proj, preferred_element_type=jnp.float32).reshape(stream.shape)
    middle = (stream.astype(jnp.float32) + projected).astype(jnp.bfloat16)
    lifted_in = layer_norm(middle).astype(jnp.bfloat16).reshape(-1, width)
    raised = jnp.dot(lifted_in, w_up, preferred_element_type=jnp.float32)
    activated = jax.nn.gelu(raised, approximate=True).astype(jnp.bfloat16)
    lowered = jnp.dot(activated, w_down, preferred_element_type=jnp.float32).reshape(stream.shape)
    return (middle.astype(jnp.float32) + lowered).astype(jnp.bfloat16)

def table_view(flat_table, level_windows):
    shaped = flat_table.reshape(level_windows, HEADS, RELPOS, -1)
    return shaped.transpose(0, 3, 1, 2)

def reference(tokens, surface_ids, surface_embed, type_index, bias_plain, bias_shift, w_qkv, w_proj, w_up, w_down):
    width = HEADS * HEAD_DIM
    levels, rows = (tokens.shape[0], tokens.shape[1])
    columns = tokens.shape[2] // width
    grid = tokens.reshape(levels, rows, columns, width)
    qkv_all = w_qkv.reshape(2, width, 3 * width)
    proj_all = w_proj.reshape(2, width, width)
    down_all = w_down.reshape(2, 4 * width, width)
    table_plain = table_view(bias_plain, levels // WZ)
    table_shift = table_view(bias_shift, levels // WZ)
    added = surface_embed[surface_ids].astype(jnp.float32)
    stream = (grid.astype(jnp.float32) + added[None]).astype(jnp.bfloat16)
    plain_labels = jnp.zeros((levels // WZ, rows // WH, WZ * WH * WW), jnp.int32)
    stream = run_block(stream, qkv_all[0], proj_all[0], w_up[0], down_all[0], table_plain, type_index, plain_labels)
    stream = jnp.roll(stream, (-(WZ // 2), -(WH // 2), -(WW // 2)), axis=(0, 1, 2))
    labels = group_labels(levels, rows, rows, 0)
    stream = run_block(stream, qkv_all[1], proj_all[1], w_up[1], down_all[1], table_shift, type_index, labels)
    stream = jnp.roll(stream, (WZ // 2, WH // 2, WW // 2), axis=(0, 1, 2))
    return stream.reshape(levels, rows, columns * width)
```

```python
import jax
import jax.numpy as jnp
import numpy as np
from jax import lax
from jax.experimental import pallas as pl
from jax.experimental.pallas import tpu as pltpu
from jax.sharding import PartitionSpec as P

HEADS = 6
HEAD_DIM = 32
C = 192
Z = 8
WZ = 2
WH = 6
WW = 12
ROWS = 12
COLS = 12
RELPOS = 3312
TYPES = 16
SPAN = 2 * WW - 1
STRIPS = 4
CELL = 144
TOKENS = 1152
HALF = 72
TABLES = 48
SHARD_ROWS = 36
KAPPA = WH * SPAN
LON = 16
BIG = 1e30
SCALE = HEAD_DIM**-0.5
PAIR = 2


def slot_positions():
    pos = np.arange(HALF)
    bh, ch, b3, c6 = pos // 36, pos // 18 % 2, pos // 6 % 3, pos % 6
    return bh * 3 + b3, ch * 6 + c6


def spread_matrix():
    b, c = slot_positions()
    out = np.zeros((2, 256, WW, 128), np.float32)
    for lane_type in range(2):
        for query_col in range(WW):
            row = b * SPAN + query_col - c + WW - 1 + lane_type * (KAPPA - 128)
            out[lane_type, row, query_col, np.arange(HALF)] = 1.0
    return out.reshape(2, 256, 6, 256).transpose(0, 2, 1, 3)


def query_tail():
    b, c = slot_positions()
    out = np.zeros((CELL, 256), np.float32)
    for a in range(2):
        rows = a * HALF + np.arange(HALF)
        out[rows, 32 + 16 * c + 8 * a + b] = 1.0
        out[rows, 224] = 1.0
        out[rows, 225 + a] = 1.0
        out[rows, 227 + b // 3] = 1.0
    return out


def mask_rows():
    b, _ = slot_positions()
    out = np.zeros((3, 32, 256), np.float32)
    for a in range(2):
        lanes = a * 128 + np.arange(HALF)
        out[0, 0, a * 128 + HALF : a * 128 + 128] = -BIG
        out[1, 1 + (1 - a), lanes] = -BIG
        out[2, 3 + (1 - b // 3), lanes] = -BIG
    return out


def head_lanes():
    out = np.zeros((HEADS, 1, C), np.float32)
    for head in range(HEADS):
        out[head, 0, head * HEAD_DIM : (head + 1) * HEAD_DIM] = 1.0
    return out


def normalised(x):
    center = jnp.sum(x, axis=-1, keepdims=True) * (1.0 / C)
    moved = x - center
    spread = jnp.sum(moved * moved, axis=-1, keepdims=True) * (1.0 / C)
    return moved * lax.rsqrt(spread + 1e-05)


def rounded(x):
    return x.astype(jnp.bfloat16).astype(jnp.float32)


def gelu(v):
    inner = v * (0.7978845608028654 + (0.7978845608028654 * 0.044715) * (v * v))
    return v * (0.5 + 0.5 * jnp.tanh(inner))


def dot(a, b):
    return jnp.dot(a, b, preferred_element_type=jnp.float32)


def dot_nt(a, b):
    return lax.dot_general(a, b, (((1,), (1,)), ((), ())), preferred_element_type=jnp.float32)


def take_strided(ref, start):
    near = ref[0, pl.ds(start, HALF, stride=8), :]
    far = ref[1, pl.ds(start, HALF, stride=8), :]
    return jnp.concatenate([near, far[:, : C - 128]], axis=1)


def put_strided(ref, start, value):
    blank = jnp.zeros((HALF, 256 - C), jnp.float32)
    ref[0, pl.ds(start, HALF, stride=8), :] = value[:, :128]
    ref[1, pl.ds(start, HALF, stride=8), :] = jnp.concatenate([value[:, 128:], blank], axis=1)


def take_rows(ref, start, count):
    return jnp.concatenate(
        [ref[0, pl.ds(start, count), :], ref[1, pl.ds(start, count), : C - 128]], axis=1
    )


def put_rows(ref, start, value):
    rows = pl.ds(start, value.shape[0])
    ref[0, rows, :] = value[:, :128]
    ref[1, rows, : C - 128] = value[:, 128:]


def spread_tables(block, gathered, spread, tables):
    for lane_type in range(2):
        left = gathered[block, :, :, 128 * lane_type : 128 * lane_type + 256].reshape(768, 256)

        def step(pair, carry):
            wide = dot(left, spread[lane_type, pair])
            wide = wide.reshape(24, 2, 2, 8, 256)
            for inner in range(2):
                for a in range(2):
                    part = wide[:, :, a, :, 128 * inner : 128 * inner + 128]
                    part = part.reshape(24, 16, 128).astype(jnp.bfloat16)
                    tables[
                        24 * lane_type : 24 * lane_type + 24,
                        2 * pair + inner,
                        :,
                        128 * a : 128 * a + 128,
                    ] = part
            return carry

        lax.fori_loop(0, 6, step, 0)


def run_block(block, x, y, tables, consts, weights, band):
    tail, masks, lanes = consts
    w_q, w_kt, w_v, w_proj, w_up, w_down = weights
    last_band = (band == lax.axis_size("lat") - 1).astype(jnp.float32) if block else None

    def step(pair, carry):
        lat_window = pair // 2
        starts, level_windows = [], []
        for i in range(PAIR):
            level_window = (pair % 2) * 2 + i
            level_windows.append(level_window)
            for a in range(2):
                level = lax.rem(2 * level_window + a + block, Z)
                starts.append(lat_window * (HALF * Z) + level)
        parts = [take_strided(x, s) for s in starts]
        stream = jnp.concatenate(parts, axis=0)
        normed = normalised(stream)
        normed_b = normed.astype(jnp.bfloat16)
        queries = dot(normed_b, w_q[block]) * SCALE
        blank = jnp.zeros((128 - HALF, C), jnp.float32)
        mixed_all = []
        for i in range(PAIR):
            first = normed[2 * i * HALF : (2 * i + 1) * HALF]
            second = normed[(2 * i + 1) * HALF : (2 * i + 2) * HALF]
            padded = jnp.concatenate([first, blank, second, blank], axis=0).astype(jnp.bfloat16)
            keys = dot_nt(w_kt[block], padded).astype(jnp.bfloat16)
            values = dot(padded, w_v[block]).astype(jnp.bfloat16)
            mask = masks[0]
            if block:
                on_level = (level_windows[i] == 3).astype(jnp.float32)
                on_lat = (lat_window == 1).astype(jnp.float32) * last_band
                mask = mask + masks[1] * on_level + masks[2] * on_lat
            mask = mask.astype(jnp.bfloat16)
            weight_parts, value_parts = [], []
            for head in range(HEADS):
                near = queries[i * CELL : (i + 1) * CELL, 128 * head : 128 * head + 128]
                near = (near + tail[:, 0:128]).astype(jnp.bfloat16)
                far = tail[:, 128:256].astype(jnp.bfloat16)
                left = jnp.concatenate([near, far], axis=1)
                table = tables[lat_window * 24 + level_windows[i] * HEADS + head].reshape(192, 256)
                right = jnp.concatenate([keys[32 * head : 32 * head + 32], table, mask], axis=0)
                scores = dot(left, right)
                top = jnp.max(scores, axis=-1, keepdims=True)
                grown = jnp.exp(scores - top)
                total = jnp.sum(grown, axis=-1, keepdims=True)
                weight_parts.append((grown * (1.0 / total)).astype(jnp.bfloat16))
                value_parts.append(values * lanes[head].astype(jnp.bfloat16))
            mixed_all.append(
                dot(jnp.concatenate(weight_parts, axis=1), jnp.concatenate(value_parts, axis=0))
            )
        mixed = jnp.concatenate(mixed_all, axis=0).astype(jnp.bfloat16)
        middle = rounded(stream + dot(mixed, w_proj[block]))
        lifted = gelu(dot(normalised(middle).astype(jnp.bfloat16), w_up[block]))
        result = middle + dot(lifted.astype(jnp.bfloat16), w_down[block])
        for j, s in enumerate(starts):
            put_strided(y, s, result[j * HALF : (j + 1) * HALF])
        return carry

    lax.fori_loop(0, 8 // PAIR, step, 0)


def kernel(
    tokens,
    ids,
    embed,
    picked,
    spread,
    tail,
    masks,
    lanes,
    w_q,
    w_kt,
    w_v,
    w_proj,
    w_up,
    w_down,
    out,
    gathered,
    tables,
    x,
    y,
    sent,
    received,
    back,
    returned,
    gather_send,
    gather_recv,
    halo_send,
    halo_recv,
):
    lat, lon = lax.axis_index("lat"), lax.axis_index("lon")
    lats, lons = lax.axis_size("lat"), lax.axis_size("lon")
    consts = (tail, masks, lanes)
    weights = (w_q, w_kt, w_v, w_proj, w_up, w_down)
    north, south = lax.rem(lat + lats - 1, lats), lax.rem(lat + 1, lats)
    west, east = lax.rem(lon + lons - 1, lons), lax.rem(lon + 1, lons)

    def place(i, j):
        return {"lat": i, "lon": j}

    barrier = pltpu.get_barrier_semaphore()
    for distance in range(1, LON):
        pl.semaphore_signal(
            barrier,
            inc=1,
            device_id=place(lat, lax.rem(lon + distance, lons)),
            device_id_type=pl.DeviceIdType.MESH,
        )
    for i, j in ((north, lon), (south, lon), (north, west), (south, east)):
        pl.semaphore_signal(
            barrier, inc=1, device_id=place(i, j), device_id_type=pl.DeviceIdType.MESH
        )
    pl.semaphore_wait(barrier, LON - 1 + 4)

    def share(block, distance, origin, target):
        return pltpu.make_async_remote_copy(
            src_ref=picked.at[block],
            dst_ref=gathered.at[block, origin],
            send_sem=gather_send.at[block, distance],
            recv_sem=gather_recv.at[block, distance],
            device_id=place(lat, target),
            device_id_type=pl.DeviceIdType.MESH,
        )

    for block in range(2):
        for distance in range(1, LON):
            share(block, distance, lon, lax.rem(lon + distance, lons)).start()
    for block in range(2):
        gathered[block, lon] = picked[block]

    def embed_row(row, carry):
        strip, inner = row // 3, row % 3
        for col in range(COLS):
            cell = tokens[row, :, C * col : C * col + C].astype(jnp.float32)
            line = embed[pl.ds(ids[row, col], 1), :]
            start = ((strip * 2 + col // 6) * 18 + inner * 6 + col % 6) * 8
            put_rows(x, pl.multiple_of(start, 8), rounded(cell + line))
        return carry

    lax.fori_loop(0, ROWS, embed_row, 0)

    def arrive(block):
        for distance in range(1, LON):
            share(block, distance, lax.rem(lon + lons - distance, lons), lon).wait_recv()

    arrive(0)
    spread_tables(0, gathered, spread, tables)
    run_block(0, x, y, tables, consts, weights, lat)

    for strip in range(STRIPS):
        for half in range(2):
            start = (strip * 2 + half) * CELL
            sent[strip, half] = take_rows(y, start, CELL).astype(jnp.bfloat16)

    def halo(index, source, target, i, j):
        return pltpu.make_async_remote_copy(
            src_ref=source,
            dst_ref=target,
            send_sem=halo_send.at[index],
            recv_sem=halo_recv.at[index],
            device_id=place(i, j),
            device_id_type=pl.DeviceIdType.MESH,
        )

    ahead = [
        halo(0, sent.at[1:4, 0], received.at[0:3], lat, west),
        halo(1, sent.at[0, 1], received.at[3], north, lon),
        halo(2, sent.at[0, 0], received.at[4], north, west),
    ]
    for copy in ahead:
        copy.start()
    arrive(1)
    spread_tables(1, gathered, spread, tables)
    for strip in range(3):
        start = strip * 2 * CELL
        put_rows(x, start, sent[strip + 1, 1].astype(jnp.float32))
    for copy in ahead:
        copy.wait()
    for strip in range(3):
        start = (strip * 2 + 1) * CELL
        put_rows(x, start, received[strip].astype(jnp.float32))
    put_rows(x, 6 * CELL, received[3].astype(jnp.float32))
    put_rows(x, 7 * CELL, received[4].astype(jnp.float32))
    run_block(1, x, y, tables, consts, weights, lat)

    for strip in range(STRIPS):
        for half in range(2):
            start = (strip * 2 + half) * CELL
            back[strip, half] = take_rows(y, start, CELL).astype(jnp.bfloat16)
    home = [
        halo(3, back.at[0:3, 1], returned.at[0:3], lat, east),
        halo(4, back.at[3, 0], returned.at[3], south, lon),
        halo(5, back.at[3, 1], returned.at[4], south, east),
    ]
    for copy in home:
        copy.start()
    for block in range(2):
        for distance in range(1, LON):
            share(block, distance, lon, lax.rem(lon + distance, lons)).wait_send()

    def put(strip, half, cells):
        for inner in range(3):
            for col in range(6):
                at = (inner * 6 + col) * 8
                lane = (half * 6 + col) * C
                out[strip * 3 + inner, :, lane : lane + C] = cells[at : at + 8].astype(jnp.bfloat16)

    for strip in range(3):
        put(strip + 1, 1, back[strip, 0].astype(jnp.float32))
    for copy in home:
        copy.wait()
    for strip in range(3):
        put(strip + 1, 0, returned[strip].astype(jnp.float32))
    put(0, 1, returned[3].astype(jnp.float32))
    put(0, 0, returned[4].astype(jnp.float32))


def pick_types(bias_plain, bias_shift, type_index):
    both = jnp.stack([bias_plain.reshape(SHARD_ROWS, -1), bias_shift.reshape(SHARD_ROWS, -1)])
    entry = jnp.arange(KAPPA * TYPES, dtype=jnp.int32)[:, None]
    lane = jnp.arange(384, dtype=jnp.int32)[None, :]
    wanted = jnp.where(lane < KAPPA, type_index[0], type_index[1])
    relative = jnp.where(lane < KAPPA, lane, lane - KAPPA)
    choose = (entry == relative * TYPES + wanted) & (lane < 2 * KAPPA)
    rows = jnp.dot(
        both.reshape(2 * SHARD_ROWS, -1),
        choose.astype(jnp.bfloat16),
        preferred_element_type=jnp.float32,
    ).astype(jnp.bfloat16)
    rows = rows.reshape(2, 6, 6, 384)
    return jnp.pad(rows, ((0, 0), (0, 0), (0, 2), (0, 0))).reshape(2, 48, 384)


def body(
    tokens,
    surface_ids,
    surface_embed,
    type_index,
    bias_plain,
    bias_shift,
    w_qkv,
    w_proj,
    w_up,
    w_down,
):
    picked = pick_types(bias_plain, bias_shift, type_index)
    qkv = w_qkv.reshape(2, C, 3 * C)
    w_q = jnp.pad(
        qkv[:, :, :C].reshape(2, C, HEADS, HEAD_DIM), ((0, 0), (0, 0), (0, 0), (0, 128 - HEAD_DIM))
    ).reshape(2, C, HEADS * 128)
    w_kt = qkv[:, :, C : 2 * C].transpose(0, 2, 1)
    w_v = qkv[:, :, 2 * C :]
    spread = jnp.asarray(spread_matrix(), jnp.bfloat16)
    tail = jnp.asarray(query_tail(), jnp.float32)
    masks = jnp.asarray(mask_rows(), jnp.float32)
    lanes = jnp.asarray(head_lanes(), jnp.float32)
    in_vmem = pl.BlockSpec(memory_space=pltpu.VMEM)
    rows = pl.pallas_call(
        kernel,
        out_shape=jax.ShapeDtypeStruct((ROWS, Z, COLS * C), jnp.bfloat16),
        in_specs=[in_vmem, pl.BlockSpec(memory_space=pltpu.SMEM)] + [in_vmem] * 12,
        out_specs=in_vmem,
        scratch_shapes=[
            pltpu.VMEM((2, LON, 48, 384), jnp.bfloat16),
            pltpu.VMEM((TABLES, WW, 16, 256), jnp.bfloat16),
            pltpu.VMEM((2, TOKENS, 128), jnp.float32),
            pltpu.VMEM((2, TOKENS, 128), jnp.float32),
            pltpu.VMEM((STRIPS, 2, CELL, C), jnp.bfloat16),
            pltpu.VMEM((5, CELL, C), jnp.bfloat16),
            pltpu.VMEM((STRIPS, 2, CELL, C), jnp.bfloat16),
            pltpu.VMEM((5, CELL, C), jnp.bfloat16),
            pltpu.SemaphoreType.DMA((2, LON)),
            pltpu.SemaphoreType.DMA((2, LON)),
            pltpu.SemaphoreType.DMA((6,)),
            pltpu.SemaphoreType.DMA((6,)),
        ],
        compiler_params=pltpu.CompilerParams(
            collective_id=0, has_side_effects=True, vmem_limit_bytes=56 * 1024 * 1024
        ),
    )(
        tokens.transpose(1, 0, 2),
        surface_ids,
        surface_embed.astype(jnp.float32),
        picked,
        spread,
        tail,
        masks,
        lanes,
        w_q,
        w_kt,
        w_v,
        w_proj.reshape(2, C, C),
        w_up,
        w_down.reshape(2, 4 * C, C),
    )
    return rows.transpose(1, 0, 2)


def solution(mesh):
    return jax.shard_map(
        body,
        mesh=mesh,
        in_specs=(
            P(None, "lat", "lon"),
            P("lat", "lon"),
            P(),
            P("lat"),
            P("lon"),
            P("lon"),
            P(),
            P(),
            P(),
            P(),
        ),
        out_specs=P(None, "lat", "lon"),
        check_vma=False,
    )
```

```python
import jax
import jax.numpy as jnp
import numpy as np
from jax import lax
from jax.experimental import pallas as pl
from jax.experimental.pallas import tpu as pltpu
from jax.sharding import PartitionSpec as P

HEADS = 6
HEAD_DIM = 32
C = 192
Z = 8
WZ = 2
WH = 6
WW = 12
ROWS = 12
COLS = 12
RELPOS = 3312
TYPES = 16
SPAN = 2 * WW - 1
STRIPS = 4
CELL = 144
TOKENS = 1152
HALF = 72
TABLES = 48
SHARD_LINES = 621
STRIDE = 69
CHUNKS = 18
KAPPA = WH * SPAN
LON = 16
BIG = 1e30
SCALE = HEAD_DIM**-0.5
PAIR = 2


def slot_positions():
    pos = np.arange(HALF)
    bh, ch, b3, c6 = pos // 36, pos // 18 % 2, pos // 6 % 3, pos % 6
    return bh * 3 + b3, ch * 6 + c6


def spread_matrix():
    b, c = slot_positions()
    out = np.zeros((2, 256, WW, 128), np.float32)
    for lane_type in range(2):
        for query_col in range(WW):
            row = b * SPAN + query_col - c + WW - 1 + lane_type * (KAPPA - 128)
            out[lane_type, row, query_col, np.arange(HALF)] = 1.0
    return out.reshape(2, 256, 6, 256).transpose(0, 2, 1, 3)


def query_tail():
    b, c = slot_positions()
    out = np.zeros((CELL, 256), np.float32)
    for a in range(2):
        rows = a * HALF + np.arange(HALF)
        out[rows, 32 + 16 * c + 8 * a + b] = 1.0
        out[rows, 224] = 1.0
        out[rows, 225 + a] = 1.0
        out[rows, 227 + b // 3] = 1.0
    return out


def mask_rows():
    b, _ = slot_positions()
    out = np.zeros((3, 32, 256), np.float32)
    for a in range(2):
        lanes = a * 128 + np.arange(HALF)
        out[0, 0, a * 128 + HALF : a * 128 + 128] = -BIG
        out[1, 1 + (1 - a), lanes] = -BIG
        out[2, 3 + (1 - b // 3), lanes] = -BIG
    return out


def head_lanes():
    out = np.zeros((HEADS, 1, C), np.float32)
    for head in range(HEADS):
        out[head, 0, head * HEAD_DIM : (head + 1) * HEAD_DIM] = 1.0
    return out


def normalised(x):
    center = jnp.sum(x, axis=-1, keepdims=True) * (1.0 / C)
    moved = x - center
    spread = jnp.sum(moved * moved, axis=-1, keepdims=True) * (1.0 / C)
    return moved * lax.rsqrt(spread + 1e-05)


def rounded(x):
    return x.astype(jnp.bfloat16).astype(jnp.float32)


def gelu(v):
    inner = v * (0.7978845608028654 + (0.7978845608028654 * 0.044715) * (v * v))
    return v * (0.5 + 0.5 * jnp.tanh(inner))


def dot(a, b):
    return jnp.dot(a, b, preferred_element_type=jnp.float32)


def dot_nt(a, b):
    return lax.dot_general(a, b, (((1,), (1,)), ((), ())), preferred_element_type=jnp.float32)


def take_strided(ref, start):
    near = ref[0, pl.ds(start, HALF, stride=8), :]
    far = ref[1, pl.ds(start, HALF, stride=8), :]
    return jnp.concatenate([near, far[:, : C - 128]], axis=1)


def put_strided(ref, start, value):
    blank = jnp.zeros((HALF, 256 - C), jnp.float32)
    ref[0, pl.ds(start, HALF, stride=8), :] = value[:, :128]
    ref[1, pl.ds(start, HALF, stride=8), :] = jnp.concatenate([value[:, 128:], blank], axis=1)


def take_rows(ref, start, count):
    return jnp.concatenate(
        [ref[0, pl.ds(start, count), :], ref[1, pl.ds(start, count), : C - 128]], axis=1
    )


def put_rows(ref, start, value):
    rows = pl.ds(start, value.shape[0])
    ref[0, rows, :] = value[:, :128]
    ref[1, rows, : C - 128] = value[:, 128:]


def pick_types(block, lines, types, choose, ordered, picked):
    lane = lax.broadcasted_iota(jnp.int32, (1, 384), 1)
    second = lane >= KAPPA
    kappa = jnp.where(second, lane - KAPPA, lane)
    for phase in range(4):
        group = jnp.where(lane < 2 * KAPPA, (kappa + 2 * phase) // 8, -1)
        left = jnp.concatenate(
            [
                lines[block, pl.ds(17 * phase + chunk, 16, stride=STRIDE), :]
                for chunk in range(CHUNKS)
            ],
            axis=0,
        ).astype(jnp.bfloat16)
        wide = dot(left, choose[phase])
        total = jnp.zeros((16, 384), jnp.float32)
        for chunk in range(CHUNKS):
            total = jnp.where(group == chunk, wide[16 * chunk : 16 * chunk + 16], total)
        for tile in range(3):
            ordered[tile, pl.ds(phase, 16, stride=4), :] = total[:, 128 * tile : 128 * tile + 128]
    row = lax.broadcasted_iota(jnp.int32, (8, 384), 0)
    groups = []
    for group in range(6):
        whole = jnp.concatenate([ordered[tile, 6 * group : 6 * group + 8, :] for tile in range(3)], axis=1)
        groups.append(jnp.where(row < 6, whole, 0.0))
    picked[block] = jnp.concatenate(groups, axis=0).astype(jnp.bfloat16)


def choose_lanes(types, choose):
    lane = lax.broadcasted_iota(jnp.int32, (1, 384), 1)
    second = lane >= KAPPA
    kappa = jnp.where(second, lane - KAPPA, lane)
    wanted = jnp.where(second, types[1], types[0])
    row = lax.broadcasted_iota(jnp.int32, (128, 384), 0)
    for phase in range(4):
        target = lax.rem(kappa + 2 * phase, 8) * TYPES + wanted
        target = jnp.where(lane < 2 * KAPPA, target, -1)
        choose[phase] = (row == target).astype(jnp.float32).astype(jnp.bfloat16)


def prepare_weights(qkv, w_q, w_kt):
    lane = lax.broadcasted_iota(jnp.int32, (1, HEADS * 128), 1)
    inner = lax.rem(lane, 128)
    target = jnp.where(inner < HEAD_DIM, (lane // 128) * HEAD_DIM + inner, -1)
    row = lax.broadcasted_iota(jnp.int32, (C, HEADS * 128), 0)
    place = (row == target).astype(jnp.float32).astype(jnp.bfloat16)
    one = lax.broadcasted_iota(jnp.int32, (C, C), 0) == lax.broadcasted_iota(jnp.int32, (C, C), 1)
    one = one.astype(jnp.float32).astype(jnp.bfloat16)
    for block in range(2):
        w_q[block] = dot(qkv[block, :, 0:C], place).astype(jnp.bfloat16)
        w_kt[block] = dot_nt(one, qkv[block, :, C : 2 * C]).astype(jnp.bfloat16)


def spread_tables(block, gathered, spread, tables):
    for lane_type in range(2):
        lanes = slice(128 * lane_type, 128 * lane_type + 256)
        left = jnp.concatenate(
            [
                gathered[block, c, x_of, z_of, :, lanes]
                for z_of in range(2)
                for x_of in range(4)
                for c in range(2)
            ],
            axis=0,
        )

        def step(pair, carry):
            wide = dot(left, spread[lane_type, pair])
            wide = wide.reshape(24, 2, 2, 8, 256)
            for inner in range(2):
                for a in range(2):
                    part = wide[:, :, a, :, 128 * inner : 128 * inner + 128]
                    part = part.reshape(24, 16, 128).astype(jnp.bfloat16)
                    tables[
                        24 * lane_type : 24 * lane_type + 24,
                        2 * pair + inner,
                        :,
                        128 * a : 128 * a + 128,
                    ] = part
            return carry

        lax.fori_loop(0, 6, step, 0)


def run_windows(block, lat_window, pair, x, y, tables, consts, weights, band):
    tail, masks, lanes = consts
    w_q, w_kt, w_v, w_proj, w_up, w_down = weights
    last_band = (band == lax.axis_size("lat") - 1).astype(jnp.float32)
    shifted = block.astype(jnp.float32)
    starts, level_windows = [], []
    for i in range(PAIR):
        level_window = pair * PAIR + i
        level_windows.append(level_window)
        for a in range(2):
            level = lax.rem(2 * level_window + a + block, Z)
            starts.append(lat_window * (HALF * Z) + level)
    parts = [take_strided(x, s) for s in starts]
    stream = jnp.concatenate(parts, axis=0)
    normed = normalised(stream)
    normed_b = normed.astype(jnp.bfloat16)
    queries = dot(normed_b, w_q[block]) * SCALE
    blank = jnp.zeros((128 - HALF, C), jnp.float32)
    mixed_all = []
    for i in range(PAIR):
        first = normed[2 * i * HALF : (2 * i + 1) * HALF]
        second = normed[(2 * i + 1) * HALF : (2 * i + 2) * HALF]
        padded = jnp.concatenate([first, blank, second, blank], axis=0).astype(jnp.bfloat16)
        keys = dot_nt(w_kt[block], padded).astype(jnp.bfloat16)
        values = dot(padded, w_v[block, :, 2 * C : 3 * C]).astype(jnp.bfloat16)
        on_level = (level_windows[i] == 3).astype(jnp.float32) * shifted
        on_lat = (lat_window == 1).astype(jnp.float32) * last_band * shifted
        mask = masks[0] + masks[1] * on_level + masks[2] * on_lat
        mask = mask.astype(jnp.bfloat16)
        weight_parts, value_parts = [], []
        for head in range(HEADS):
            near = queries[i * CELL : (i + 1) * CELL, 128 * head : 128 * head + 128]
            near = (near + tail[:, 0:128]).astype(jnp.bfloat16)
            far = tail[:, 128:256].astype(jnp.bfloat16)
            left = jnp.concatenate([near, far], axis=1)
            table = tables[lat_window * 24 + level_windows[i] * HEADS + head].reshape(192, 256)
            right = jnp.concatenate([keys[32 * head : 32 * head + 32], table, mask], axis=0)
            scores = dot(left, right)
            top = jnp.max(scores, axis=-1, keepdims=True)
            grown = jnp.exp(scores - top)
            total = jnp.sum(grown, axis=-1, keepdims=True)
            weight_parts.append((grown * (1.0 / total)).astype(jnp.bfloat16))
            value_parts.append(values * lanes[head].astype(jnp.bfloat16))
        mixed_all.append(
            dot(jnp.concatenate(weight_parts, axis=1), jnp.concatenate(value_parts, axis=0))
        )
    mixed = jnp.concatenate(mixed_all, axis=0).astype(jnp.bfloat16)
    middle = rounded(stream + dot(mixed, w_proj[block]))
    lifted = gelu(dot(normalised(middle).astype(jnp.bfloat16), w_up[block]))
    result = middle + dot(lifted.astype(jnp.bfloat16), w_down[block])
    for j, s in enumerate(starts):
        put_strided(y, s, result[j * HALF : (j + 1) * HALF])


def kernel(
    tokens_hbm,
    ids,
    types,
    embed_in,
    bias_plain,
    bias_shift,
    spread_hbm,
    tail,
    masks,
    lanes,
    qkv_hbm,
    proj_hbm,
    up_hbm,
    down_hbm,
    out,
    tokens,
    embed,
    lines,
    choose,
    ordered,
    picked,
    spread,
    qkv,
    w_q,
    w_kt,
    w_proj,
    w_up,
    w_down,
    gathered,
    tables,
    x,
    y,
    sent,
    received,
    back,
    returned,
    local_sems,
    gather_send,
    gather_recv,
    halo_send,
    halo_recv,
):
    lat, lon = lax.axis_index("lat"), lax.axis_index("lon")
    lats, lons = lax.axis_size("lat"), lax.axis_size("lon")
    consts = (tail, masks, lanes)
    weights = (w_q, w_kt, qkv, w_proj, w_up, w_down)
    north, south = lax.rem(lat + lats - 1, lats), lax.rem(lat + 1, lats)
    west, east = lax.rem(lon + lons - 1, lons), lax.rem(lon + 1, lons)

    sources = (tokens_hbm, qkv_hbm, spread_hbm, proj_hbm, up_hbm, down_hbm)
    targets = (tokens, qkv, spread, w_proj, w_up, w_down)
    loads = [
        pltpu.make_async_copy(source, target, local_sems.at[i])
        for i, (source, target) in enumerate(zip(sources, targets))
    ]
    for load in loads:
        load.start()

    def place(i, j):
        return {"lat": i, "lon": j}

    crosses, sides = 2, 2
    across = lons // (crosses * sides)
    core, x_at, z_at = lax.rem(lon, sides), lax.rem(lon // sides, across), lon // (sides * across)

    def lon_of(z, x, c):
        return (z * across + x) * sides + c

    opposite = lon_of(1 - z_at, x_at, core)
    sibling = lon_of(z_at, x_at, 1 - core)
    peers = [lon_of(z_at, lax.rem(x_at + step, across), core) for step in range(1, 4)]
    origins = [lax.rem(x_at + across - step, across) for step in range(1, 4)]
    partners = [(lat, j) for j in (opposite, sibling, *peers, west, east)]
    partners += [(north, lon), (south, lon), (north, west), (south, east)]

    barrier = pltpu.get_barrier_semaphore()
    for i, j in partners:
        pl.semaphore_signal(
            barrier, inc=1, device_id=place(i, j), device_id_type=pl.DeviceIdType.MESH
        )

    def share(block, index, source, slot, target):
        return pltpu.make_async_remote_copy(
            src_ref=source,
            dst_ref=slot,
            send_sem=gather_send.at[block, index],
            recv_sem=gather_recv.at[block, index],
            device_id=place(lat, target),
            device_id_type=pl.DeviceIdType.MESH,
        )

    def slot(block, x_of, z_of):
        return gathered.at[block, core, x_of, z_of]

    def own_copy(block, i):
        target = opposite if i == 0 else peers[i - 1]
        return share(block, i, picked.at[block], slot(block, x_at, z_at), target)

    def passed_copy(block, i):
        held = slot(block, x_at, 1 - z_at)
        return share(block, 4 + i, held, held, peers[i])

    def sibling_copy(block):
        held = gathered.at[block, core]
        return share(block, 7, held, held, sibling)

    def wait_opposite(block):
        share(block, 0, picked.at[block], slot(block, x_at, 1 - z_at), opposite).wait_recv()

    def wait_peers(block):
        for i, origin in enumerate(origins):
            share(block, 1 + i, picked.at[block], slot(block, origin, z_at), lon).wait_recv()
        for i, origin in enumerate(origins):
            share(block, 4 + i, picked.at[block], slot(block, origin, 1 - z_at), lon).wait_recv()

    def wait_sibling(block):
        other = gathered.at[block, 1 - core]
        share(block, 7, other, other, sibling).wait_recv()

    lines[0, 0:SHARD_LINES] = bias_plain[...].astype(jnp.float32)
    lines[1, 0:SHARD_LINES] = bias_shift[...].astype(jnp.float32)
    choose_lanes(types, choose)
    pl.semaphore_wait(barrier, len(partners))

    def pick_and_send(block, carry):
        pick_types(block, lines, types, choose, ordered, picked)
        for i in range(4):
            own_copy(block, i).start()
        gathered[block, core, x_at, z_at] = picked[block]
        return carry

    lax.fori_loop(0, 2, pick_and_send, 0)

    embed[0:3, :] = embed_in[...].astype(jnp.float32)
    loads[0].wait()

    def embed_row(row, carry):
        strip, inner = row // 3, row % 3
        for col in range(COLS):
            cell = tokens[row, :, C * col : C * col + C].astype(jnp.float32)
            line = embed[pl.ds(ids[row, col], 1), :]
            start = ((strip * 2 + col // 6) * 18 + inner * 6 + col % 6) * 8
            put_rows(x, pl.multiple_of(start, 8), rounded(cell + line))
        return carry

    lax.fori_loop(0, ROWS, embed_row, 0)

    def pass_on(block):
        wait_opposite(block)
        for i in range(3):
            passed_copy(block, i).start()

    pass_on(0)
    loads[1].wait()
    prepare_weights(qkv, w_q, w_kt)
    pass_on(1)
    wait_peers(0)
    sibling_copy(0).start()
    for load in loads[2:]:
        load.wait()

    def halo(index, source, target, i, j):
        return pltpu.make_async_remote_copy(
            src_ref=source,
            dst_ref=target,
            send_sem=halo_send.at[index],
            recv_sem=halo_recv.at[index],
            device_id=place(i, j),
            device_id_type=pl.DeviceIdType.MESH,
        )

    ahead = [
        halo(0, sent.at[0, 0], received.at[4], north, west),
        halo(1, sent.at[0, 1], received.at[3], north, lon),
        halo(2, sent.at[1, 0], received.at[0], lat, west),
        halo(3, sent.at[3, 0], received.at[2], lat, west),
        halo(4, sent.at[2, 0], received.at[1], lat, west),
    ]
    home = [
        halo(5, back.at[3, 1], returned.at[4], south, east),
        halo(6, back.at[3, 0], returned.at[3], south, lon),
        halo(7, back.at[2, 1], returned.at[2], lat, east),
        halo(8, back.at[0:2, 1], returned.at[0:2], lat, east),
    ]

    def narrow(target, strips):
        for strip in strips:
            for half in range(2):
                start = (strip * 2 + half) * CELL
                target[strip, half] = take_rows(y, start, CELL).astype(jnp.bfloat16)

    def widen(strip, half, source):
        put_rows(x, (strip * 2 + half) * CELL, source.astype(jnp.float32))

    def step(at, carry):
        stage, pair = at // 2, lax.rem(at, 2)
        block = stage // 2
        lat_window = jnp.where(block == 0, stage, 3 - stage)

        @pl.when(lax.rem(at, 4) == 0)
        def _():
            wait_sibling(block)
            spread_tables(block, gathered, spread, tables)

        @pl.when(at == 4)
        def _():
            widen(2, 0, sent[3, 1])
            for i in (3, 1, 0):
                ahead[i].wait_recv()
            widen(2, 1, received[2])
            widen(3, 0, received[3])
            widen(3, 1, received[4])

        @pl.when(at == 6)
        def _():
            widen(0, 0, sent[1, 1])
            widen(1, 0, sent[2, 1])
            ahead[2].wait_recv()
            ahead[4].wait_recv()
            widen(0, 1, received[0])
            widen(1, 1, received[1])

        run_windows(block, lat_window, pair, x, y, tables, consts, weights, lat)

        @pl.when(at == 1)
        def _():
            narrow(sent, (0, 1))
            for i in (0, 1, 2):
                ahead[i].start()
            wait_peers(1)
            sibling_copy(1).start()

        @pl.when(at == 3)
        def _():
            narrow(sent, (2, 3))
            for i in (3, 4):
                ahead[i].start()

        @pl.when(at == 5)
        def _():
            narrow(back, (2, 3))
            for i in (0, 1, 2):
                home[i].start()

        @pl.when(at == 7)
        def _():
            narrow(back, (0, 1))
            home[3].start()

        return carry

    lax.fori_loop(0, 8, step, 0)

    def put(strip, half, cells):
        for inner in range(3):
            for col in range(6):
                at = (inner * 6 + col) * 8
                lane = (half * 6 + col) * C
                out[strip * 3 + inner, :, lane : lane + C] = cells[at : at + 8].astype(jnp.bfloat16)

    for strip in range(3):
        put(strip + 1, 1, back[strip, 0].astype(jnp.float32))
    for copy in ahead:
        copy.wait_send()
    for block in range(2):
        for i in range(4):
            own_copy(block, i).wait_send()
        for i in range(3):
            passed_copy(block, i).wait_send()
        sibling_copy(block).wait_send()
    for copy in home[:3]:
        copy.wait()
    put(3, 0, returned[2].astype(jnp.float32))
    put(0, 1, returned[3].astype(jnp.float32))
    put(0, 0, returned[4].astype(jnp.float32))
    home[3].wait()
    for strip in range(2):
        put(strip + 1, 0, returned[strip].astype(jnp.float32))


def body(
    tokens,
    surface_ids,
    surface_embed,
    type_index,
    bias_plain,
    bias_shift,
    w_qkv,
    w_proj,
    w_up,
    w_down,
):
    spread = jnp.asarray(spread_matrix(), jnp.bfloat16)
    tail = jnp.asarray(query_tail(), jnp.float32)
    masks = jnp.asarray(mask_rows(), jnp.float32)
    lanes = jnp.asarray(head_lanes(), jnp.float32)
    in_vmem = pl.BlockSpec(memory_space=pltpu.VMEM)
    in_smem = pl.BlockSpec(memory_space=pltpu.SMEM)
    anywhere = pl.BlockSpec(memory_space=pl.ANY)
    rows = pl.pallas_call(
        kernel,
        out_shape=jax.ShapeDtypeStruct((ROWS, Z, COLS * C), jnp.bfloat16),
        in_specs=[anywhere, in_smem, in_smem]
        + [in_vmem] * 3
        + [anywhere]
        + [in_vmem] * 3
        + [anywhere] * 4,
        out_specs=in_vmem,
        scratch_shapes=[
            pltpu.VMEM((ROWS, Z, COLS * C), jnp.bfloat16),
            pltpu.VMEM((8, C), jnp.float32),
            pltpu.VMEM((2, 1104, 128), jnp.float32),
            pltpu.VMEM((4, 128, 384), jnp.bfloat16),
            pltpu.VMEM((3, 64, 128), jnp.float32),
            pltpu.VMEM((2, 48, 384), jnp.bfloat16),
            pltpu.VMEM((2, 6, 256, 256), jnp.bfloat16),
            pltpu.VMEM((2, C, 3 * C), jnp.bfloat16),
            pltpu.VMEM((2, C, HEADS * 128), jnp.bfloat16),
            pltpu.VMEM((2, C, C), jnp.bfloat16),
            pltpu.VMEM((2, C, C), jnp.bfloat16),
            pltpu.VMEM((2, C, 4 * C), jnp.bfloat16),
            pltpu.VMEM((2, 4 * C, C), jnp.bfloat16),
            pltpu.VMEM((2, 2, 4, 2, 48, 384), jnp.bfloat16),
            pltpu.VMEM((TABLES, WW, 16, 256), jnp.bfloat16),
            pltpu.VMEM((2, TOKENS, 128), jnp.float32),
            pltpu.VMEM((2, TOKENS, 128), jnp.float32),
            pltpu.VMEM((STRIPS, 2, CELL, C), jnp.bfloat16),
            pltpu.VMEM((5, CELL, C), jnp.bfloat16),
            pltpu.VMEM((STRIPS, 2, CELL, C), jnp.bfloat16),
            pltpu.VMEM((5, CELL, C), jnp.bfloat16),
            pltpu.SemaphoreType.DMA((6,)),
            pltpu.SemaphoreType.DMA((2, 8)),
            pltpu.SemaphoreType.DMA((2, 8)),
            pltpu.SemaphoreType.DMA((9,)),
            pltpu.SemaphoreType.DMA((9,)),
        ],
        compiler_params=pltpu.CompilerParams(
            collective_id=0, has_side_effects=True, vmem_limit_bytes=56 * 1024 * 1024
        ),
    )(
        tokens.transpose(1, 0, 2),
        surface_ids,
        type_index,
        surface_embed,
        bias_plain.reshape(SHARD_LINES, 128),
        bias_shift.reshape(SHARD_LINES, 128),
        spread,
        tail,
        masks,
        lanes,
        w_qkv.reshape(2, C, 3 * C),
        w_proj.reshape(2, C, C),
        w_up,
        w_down.reshape(2, 4 * C, C),
    )
    return rows.transpose(1, 0, 2)


def solution(mesh):
    return jax.shard_map(
        body,
        mesh=mesh,
        in_specs=(
            P(None, "lat", "lon"),
            P("lat", "lon"),
            P(),
            P("lat"),
            P("lon"),
            P("lon"),
            P(),
            P(),
            P(),
            P(),
        ),
        out_specs=P(None, "lat", "lon"),
        check_vma=False,
    )
```

```python
import jax
import jax.numpy as jnp
import numpy as np
from jax import lax
from jax.experimental import pallas as pl
from jax.experimental.pallas import tpu as pltpu
from jax.sharding import PartitionSpec as P

HEADS = 6
HEAD_DIM = 32
C = 192
Z = 8
WZ = 2
WH = 6
WW = 12
ROWS = 12
COLS = 12
RELPOS = 3312
TYPES = 16
SPAN = 2 * WW - 1
STRIPS = 4
CELL = 144
TOKENS = 1152
HALF = 72
TABLES = 48
SHARD_LINES = 621
STRIDE = 69
CHUNKS = 18
KAPPA = WH * SPAN
LON = 16
BIG = 1e30
SCALE = HEAD_DIM**-0.5
PAIR = 2


def slot_positions():
    pos = np.arange(HALF)
    bh, ch, b3, c6 = pos // 36, pos // 18 % 2, pos // 6 % 3, pos % 6
    return bh * 3 + b3, ch * 6 + c6


def spread_matrix():
    b, c = slot_positions()
    out = np.zeros((2, 256, WW, 128), np.float32)
    for lane_type in range(2):
        for query_col in range(WW):
            row = b * SPAN + query_col - c + WW - 1 + lane_type * (KAPPA - 128)
            out[lane_type, row, query_col, np.arange(HALF)] = 1.0
    return out.reshape(2, 256, 6, 256).transpose(0, 2, 1, 3)


def query_tail():
    b, c = slot_positions()
    out = np.zeros((CELL, 256), np.float32)
    for a in range(2):
        rows = a * HALF + np.arange(HALF)
        out[rows, 32 + 16 * c + 8 * a + b] = 1.0
        out[rows, 224] = 1.0
        out[rows, 225 + a] = 1.0
        out[rows, 227 + b // 3] = 1.0
    return out


def mask_rows():
    b, _ = slot_positions()
    out = np.zeros((3, 32, 256), np.float32)
    for a in range(2):
        lanes = a * 128 + np.arange(HALF)
        out[0, 0, a * 128 + HALF : a * 128 + 128] = -BIG
        out[1, 1 + (1 - a), lanes] = -BIG
        out[2, 3 + (1 - b // 3), lanes] = -BIG
    return out


def head_lanes():
    out = np.zeros((HEADS + 1, 1, 256), np.float32)
    for head in range(HEADS):
        out[head, 0, head * HEAD_DIM : (head + 1) * HEAD_DIM] = 1.0
        out[head, 0, C + head] = 1.0
        out[HEADS, 0, C + head] = 1.0
    return out


def head_spread():
    out = np.zeros((256, C), np.float32)
    for head in range(HEADS):
        for row in (64 + head, 192 + head):
            out[row, head * HEAD_DIM : (head + 1) * HEAD_DIM] = 1.0
    return out


def normalised(x):
    center = jnp.sum(x, axis=-1, keepdims=True) * (1.0 / C)
    moved = x - center
    spread = jnp.sum(moved * moved, axis=-1, keepdims=True) * (1.0 / C)
    return moved * lax.rsqrt(spread + 1e-05)


def rounded(x):
    return x.astype(jnp.bfloat16).astype(jnp.float32)


def gelu(v):
    v = v.astype(jnp.bfloat16)
    first, third = jnp.bfloat16(0.7978845608028654), jnp.bfloat16(0.7978845608028654 * 0.044715)
    grown = jnp.tanh(v * (first + third * (v * v)))
    half = jnp.bfloat16(0.5) * v
    return half + half * grown


def dot(a, b):
    return jnp.dot(a, b, preferred_element_type=jnp.float32)


def dot_nt(a, b):
    return lax.dot_general(a, b, (((1,), (1,)), ((), ())), preferred_element_type=jnp.float32)


def take_strided(ref, start):
    near = ref[0, pl.ds(start, HALF, stride=8), :]
    far = ref[1, pl.ds(start, HALF, stride=8), :]
    return jnp.concatenate([near, far[:, : C - 128]], axis=1)


def put_strided(ref, start, value):
    blank = jnp.zeros((HALF, 256 - C), jnp.float32)
    ref[0, pl.ds(start, HALF, stride=8), :] = value[:, :128]
    ref[1, pl.ds(start, HALF, stride=8), :] = jnp.concatenate([value[:, 128:], blank], axis=1)


def take_rows(ref, start, count):
    return jnp.concatenate(
        [ref[0, pl.ds(start, count), :], ref[1, pl.ds(start, count), : C - 128]], axis=1
    )


def put_rows(ref, start, value):
    rows = pl.ds(start, value.shape[0])
    ref[0, rows, :] = value[:, :128]
    ref[1, rows, : C - 128] = value[:, 128:]


def pick_types(block, lines, types, choose, ordered, picked):
    lane = lax.broadcasted_iota(jnp.int32, (1, 384), 1)
    second = lane >= KAPPA
    kappa = jnp.where(second, lane - KAPPA, lane)
    for phase in range(4):
        group = jnp.where(lane < 2 * KAPPA, (kappa + 2 * phase) // 8, -1)
        left = jnp.concatenate(
            [
                lines[block, pl.ds(17 * phase + chunk, 16, stride=STRIDE), :]
                for chunk in range(CHUNKS)
            ],
            axis=0,
        ).astype(jnp.bfloat16)
        wide = dot(left, choose[phase])
        total = jnp.zeros((16, 384), jnp.float32)
        for chunk in range(CHUNKS):
            total = jnp.where(group == chunk, wide[16 * chunk : 16 * chunk + 16], total)
        for tile in range(3):
            ordered[tile, pl.ds(phase, 16, stride=4), :] = total[:, 128 * tile : 128 * tile + 128]
    row = lax.broadcasted_iota(jnp.int32, (8, 384), 0)
    groups = []
    for group in range(6):
        whole = jnp.concatenate([ordered[tile, 6 * group : 6 * group + 8, :] for tile in range(3)], axis=1)
        groups.append(jnp.where(row < 6, whole, 0.0))
    picked[block] = jnp.concatenate(groups, axis=0).astype(jnp.bfloat16)


def choose_lanes(types, choose):
    lane = lax.broadcasted_iota(jnp.int32, (1, 384), 1)
    second = lane >= KAPPA
    kappa = jnp.where(second, lane - KAPPA, lane)
    wanted = jnp.where(second, types[1], types[0])
    row = lax.broadcasted_iota(jnp.int32, (128, 384), 0)
    for phase in range(4):
        target = lax.rem(kappa + 2 * phase, 8) * TYPES + wanted
        target = jnp.where(lane < 2 * KAPPA, target, -1)
        choose[phase] = (row == target).astype(jnp.float32).astype(jnp.bfloat16)


def prepare_weights(qkv, w_q, w_kt, w_v):
    lane = lax.broadcasted_iota(jnp.int32, (1, HEADS * 128), 1)
    inner = lax.rem(lane, 128)
    target = jnp.where(inner < HEAD_DIM, (lane // 128) * HEAD_DIM + inner, -1)
    row = lax.broadcasted_iota(jnp.int32, (C, HEADS * 128), 0)
    place = (row == target).astype(jnp.float32).astype(jnp.bfloat16)
    one = lax.broadcasted_iota(jnp.int32, (C, C), 0) == lax.broadcasted_iota(jnp.int32, (C, C), 1)
    one = one.astype(jnp.float32).astype(jnp.bfloat16)
    for block in range(2):
        w_q[block] = dot(qkv[block, :, 0:C], place).astype(jnp.bfloat16)
        w_kt[block] = dot_nt(one, qkv[block, :, C : 2 * C]).astype(jnp.bfloat16)
        blank = jnp.zeros((C, 256 - C), jnp.bfloat16)
        w_v[block] = jnp.concatenate([qkv[block, :, 2 * C : 3 * C], blank], axis=1)


def spread_tables(block, gathered, spread, tables):
    for lane_type in range(2):
        lanes = slice(128 * lane_type, 128 * lane_type + 256)
        left = jnp.concatenate(
            [
                gathered[block, c, x_of, z_of, :, lanes]
                for z_of in range(2)
                for x_of in range(4)
                for c in range(2)
            ],
            axis=0,
        )

        def step(pair, carry):
            wide = dot(left, spread[lane_type, pair])
            wide = wide.reshape(24, 2, 2, 8, 256)
            for inner in range(2):
                for a in range(2):
                    part = wide[:, :, a, :, 128 * inner : 128 * inner + 128]
                    part = part.reshape(24, 16, 128).astype(jnp.bfloat16)
                    tables[
                        24 * lane_type : 24 * lane_type + 24,
                        2 * pair + inner,
                        :,
                        128 * a : 128 * a + 128,
                    ] = part
            return carry

        lax.fori_loop(0, 6, step, 0)


def run_windows(block, lat_window, pair, x, y, tables, consts, weights, band):
    tail, masks, lanes, across_heads = consts
    w_q, w_kt, w_v, w_proj, w_up, w_down = weights
    last_band = (band == lax.axis_size("lat") - 1).astype(jnp.float32)
    shifted = block.astype(jnp.float32)
    starts, level_windows = [], []
    for i in range(PAIR):
        level_window = pair * PAIR + i
        level_windows.append(level_window)
        for a in range(2):
            level = lax.rem(2 * level_window + a + block, Z)
            starts.append(lat_window * (HALF * Z) + level)
    parts = [take_strided(x, s) for s in starts]
    stream = jnp.concatenate(parts, axis=0)
    normed = normalised(stream)
    normed_b = normed.astype(jnp.bfloat16)
    queries = dot(normed_b, w_q[block]) * SCALE
    blank = jnp.zeros((128 - HALF, C), jnp.float32)
    mixed_all = []
    for i in range(PAIR):
        first = normed[2 * i * HALF : (2 * i + 1) * HALF]
        second = normed[(2 * i + 1) * HALF : (2 * i + 2) * HALF]
        padded = jnp.concatenate([first, blank, second, blank], axis=0).astype(jnp.bfloat16)
        keys = dot_nt(w_kt[block], padded).astype(jnp.bfloat16)
        values = (dot(padded, w_v[block]) + lanes[HEADS]).astype(jnp.bfloat16)
        on_level = (level_windows[i] == 3).astype(jnp.float32) * shifted
        on_lat = (lat_window == 1).astype(jnp.float32) * last_band * shifted
        mask = masks[0] + masks[1] * on_level + masks[2] * on_lat
        mask = mask.astype(jnp.bfloat16)
        weight_parts, value_parts = [], []
        for head in range(HEADS):
            near = queries[i * CELL : (i + 1) * CELL, 128 * head : 128 * head + 128]
            near = (near + tail[:, 0:128]).astype(jnp.bfloat16)
            far = tail[:, 128:256].astype(jnp.bfloat16)
            left = jnp.concatenate([near, far], axis=1)
            table = tables[lat_window * 24 + level_windows[i] * HEADS + head].reshape(192, 256)
            right = jnp.concatenate([keys[32 * head : 32 * head + 32], table, mask], axis=0)
            scores = dot(left, right)
            top = jnp.max(scores, axis=-1, keepdims=True)
            weight_parts.append(jnp.exp((scores - top).astype(jnp.bfloat16)))
            value_parts.append(values * lanes[head].astype(jnp.bfloat16))
        mixed_all.append(
            dot(jnp.concatenate(weight_parts, axis=1), jnp.concatenate(value_parts, axis=0))
        )
    mixed = jnp.concatenate(mixed_all, axis=0)
    totals = mixed[:, 128:256]
    lane = lax.broadcasted_iota(jnp.int32, totals.shape, 1)
    counted = (lane >= C - 128) & (lane < C - 128 + HEADS)
    inverse = jnp.where(counted, 1.0 / totals, 0.0)
    coarse = inverse.astype(jnp.bfloat16)
    fine = (inverse - coarse.astype(jnp.float32)).astype(jnp.bfloat16)
    scale = dot(jnp.concatenate([coarse, fine], axis=1), across_heads[...])
    mixed = (mixed[:, :C] * scale).astype(jnp.bfloat16)
    middle = rounded(stream + dot(mixed, w_proj[block]))
    lifted = gelu(dot(normalised(middle).astype(jnp.bfloat16), w_up[block]))
    result = middle + dot(lifted, w_down[block])
    for j, s in enumerate(starts):
        put_strided(y, s, result[j * HALF : (j + 1) * HALF])


def kernel(
    tokens_hbm,
    ids,
    types,
    embed_in,
    bias_plain,
    bias_shift,
    spread_hbm,
    tail,
    masks,
    lanes,
    across_heads,
    qkv_hbm,
    proj_hbm,
    up_hbm,
    down_hbm,
    out,
    tokens,
    embed,
    lines,
    choose,
    ordered,
    picked,
    spread,
    qkv,
    w_q,
    w_kt,
    w_v,
    w_proj,
    w_up,
    w_down,
    gathered,
    tables,
    x,
    y,
    sent,
    received,
    back,
    returned,
    local_sems,
    gather_send,
    gather_recv,
    halo_send,
    halo_recv,
):
    lat, lon = lax.axis_index("lat"), lax.axis_index("lon")
    lats, lons = lax.axis_size("lat"), lax.axis_size("lon")
    consts = (tail, masks, lanes, across_heads)
    weights = (w_q, w_kt, w_v, w_proj, w_up, w_down)
    north, south = lax.rem(lat + lats - 1, lats), lax.rem(lat + 1, lats)
    west, east = lax.rem(lon + lons - 1, lons), lax.rem(lon + 1, lons)

    sources = (tokens_hbm, qkv_hbm, spread_hbm, proj_hbm, up_hbm, down_hbm)
    targets = (tokens, qkv, spread, w_proj, w_up, w_down)
    loads = [
        pltpu.make_async_copy(source, target, local_sems.at[i])
        for i, (source, target) in enumerate(zip(sources, targets))
    ]
    for load in loads:
        load.start()

    def place(i, j):
        return {"lat": i, "lon": j}

    crosses, sides = 2, 2
    across = lons // (crosses * sides)
    core, x_at, z_at = lax.rem(lon, sides), lax.rem(lon // sides, across), lon // (sides * across)

    def lon_of(z, x, c):
        return (z * across + x) * sides + c

    opposite = lon_of(1 - z_at, x_at, core)
    sibling = lon_of(z_at, x_at, 1 - core)
    peers = [lon_of(z_at, lax.rem(x_at + step, across), core) for step in range(1, 4)]
    origins = [lax.rem(x_at + across - step, across) for step in range(1, 4)]
    partners = [(lat, j) for j in (opposite, sibling, *peers, west, east)]
    partners += [(north, lon), (south, lon), (north, west), (south, east)]

    barrier = pltpu.get_barrier_semaphore()
    for i, j in partners:
        pl.semaphore_signal(
            barrier, inc=1, device_id=place(i, j), device_id_type=pl.DeviceIdType.MESH
        )

    def share(block, index, source, slot, target):
        return pltpu.make_async_remote_copy(
            src_ref=source,
            dst_ref=slot,
            send_sem=gather_send.at[block, index],
            recv_sem=gather_recv.at[block, index],
            device_id=place(lat, target),
            device_id_type=pl.DeviceIdType.MESH,
        )

    def slot(block, x_of, z_of):
        return gathered.at[block, core, x_of, z_of]

    def own_copy(block, i):
        target = opposite if i == 0 else peers[i - 1]
        return share(block, i, picked.at[block], slot(block, x_at, z_at), target)

    def passed_copy(block, i):
        held = slot(block, x_at, 1 - z_at)
        return share(block, 4 + i, held, held, peers[i])

    def sibling_copy(block):
        held = gathered.at[block, core]
        return share(block, 7, held, held, sibling)

    def wait_opposite(block):
        share(block, 0, picked.at[block], slot(block, x_at, 1 - z_at), opposite).wait_recv()

    def wait_peers(block):
        for i, origin in enumerate(origins):
            share(block, 1 + i, picked.at[block], slot(block, origin, z_at), lon).wait_recv()
        for i, origin in enumerate(origins):
            share(block, 4 + i, picked.at[block], slot(block, origin, 1 - z_at), lon).wait_recv()

    def wait_sibling(block):
        other = gathered.at[block, 1 - core]
        share(block, 7, other, other, sibling).wait_recv()

    lines[0, 0:SHARD_LINES] = bias_plain[...].astype(jnp.float32)
    lines[1, 0:SHARD_LINES] = bias_shift[...].astype(jnp.float32)
    choose_lanes(types, choose)
    pl.semaphore_wait(barrier, len(partners))

    def pick_and_send(block):
        pick_types(block, lines, types, choose, ordered, picked)
        for i in range(4):
            own_copy(block, i).start()
        gathered[block, core, x_at, z_at] = picked[block]

    pick_and_send(0)

    embed[0:3, :] = embed_in[...].astype(jnp.float32)
    loads[0].wait()

    def embed_row(row, carry):
        strip, inner = row // 3, row % 3
        for col in range(COLS):
            cell = tokens[row, :, C * col : C * col + C].astype(jnp.float32)
            line = embed[pl.ds(ids[row, col], 1), :]
            start = ((strip * 2 + col // 6) * 18 + inner * 6 + col % 6) * 8
            put_rows(x, pl.multiple_of(start, 8), rounded(cell + line))
        return carry

    lax.fori_loop(0, ROWS, embed_row, 0)

    def pass_on(block):
        wait_opposite(block)
        for i in range(3):
            passed_copy(block, i).start()

    pass_on(0)
    loads[1].wait()
    prepare_weights(qkv, w_q, w_kt, w_v)
    wait_peers(0)
    sibling_copy(0).start()
    pick_and_send(1)
    for load in loads[2:]:
        load.wait()

    def halo(index, source, target, i, j):
        return pltpu.make_async_remote_copy(
            src_ref=source,
            dst_ref=target,
            send_sem=halo_send.at[index],
            recv_sem=halo_recv.at[index],
            device_id=place(i, j),
            device_id_type=pl.DeviceIdType.MESH,
        )

    ahead = [
        halo(0, sent.at[0, 0], received.at[4], north, west),
        halo(1, sent.at[0, 1], received.at[3], north, lon),
        halo(2, sent.at[1, 0], received.at[0], lat, west),
        halo(3, sent.at[3, 0], received.at[2], lat, west),
        halo(4, sent.at[2, 0], received.at[1], lat, west),
    ]
    home = [
        halo(5, back.at[3, 1], returned.at[4], south, east),
        halo(6, back.at[3, 0], returned.at[3], south, lon),
        halo(7, back.at[2, 1], returned.at[2], lat, east),
        halo(8, back.at[0:2, 1], returned.at[0:2], lat, east),
    ]

    def narrow(target, strips):
        for strip in strips:
            for half in range(2):
                start = (strip * 2 + half) * CELL
                target[strip, half] = take_rows(y, start, CELL).astype(jnp.bfloat16)

    def widen(strip, half, source):
        put_rows(x, (strip * 2 + half) * CELL, source.astype(jnp.float32))

    def step(at, carry):
        stage, pair = at // 2, lax.rem(at, 2)
        block = stage // 2
        lat_window = jnp.where(block == 0, stage, 3 - stage)

        @pl.when(lax.rem(at, 4) == 0)
        def _():
            wait_sibling(block)
            spread_tables(block, gathered, spread, tables)

        @pl.when(at == 4)
        def _():
            widen(2, 0, sent[3, 1])
            for i in (3, 1, 0):
                ahead[i].wait_recv()
            widen(2, 1, received[2])
            widen(3, 0, received[3])
            widen(3, 1, received[4])

        @pl.when(at == 6)
        def _():
            widen(0, 0, sent[1, 1])
            widen(1, 0, sent[2, 1])
            ahead[2].wait_recv()
            ahead[4].wait_recv()
            widen(0, 1, received[0])
            widen(1, 1, received[1])

        run_windows(block, lat_window, pair, x, y, tables, consts, weights, lat)

        @pl.when(at == 0)
        def _():
            pass_on(1)

        @pl.when(at == 1)
        def _():
            narrow(sent, (0, 1))
            for i in (0, 1, 2):
                ahead[i].start()
            wait_peers(1)
            sibling_copy(1).start()

        @pl.when(at == 3)
        def _():
            narrow(sent, (2, 3))
            for i in (3, 4):
                ahead[i].start()

        @pl.when(at == 5)
        def _():
            narrow(back, (2, 3))
            for i in (0, 1, 2):
                home[i].start()

        @pl.when(at == 7)
        def _():
            narrow(back, (0, 1))
            home[3].start()

        return carry

    lax.fori_loop(0, 8, step, 0)

    def put(strip, half, cells):
        for inner in range(3):
            for col in range(6):
                at = (inner * 6 + col) * 8
                lane = (half * 6 + col) * C
                out[strip * 3 + inner, :, lane : lane + C] = cells[at : at + 8].astype(jnp.bfloat16)

    for strip in range(3):
        put(strip + 1, 1, back[strip, 0].astype(jnp.float32))
    for copy in ahead:
        copy.wait_send()
    for block in range(2):
        for i in range(4):
            own_copy(block, i).wait_send()
        for i in range(3):
            passed_copy(block, i).wait_send()
        sibling_copy(block).wait_send()
    for copy in home[:3]:
        copy.wait()
    put(3, 0, returned[2].astype(jnp.float32))
    put(0, 1, returned[3].astype(jnp.float32))
    put(0, 0, returned[4].astype(jnp.float32))
    home[3].wait()
    for strip in range(2):
        put(strip + 1, 0, returned[strip].astype(jnp.float32))


def body(
    tokens,
    surface_ids,
    surface_embed,
    type_index,
    bias_plain,
    bias_shift,
    w_qkv,
    w_proj,
    w_up,
    w_down,
):
    spread = jnp.asarray(spread_matrix(), jnp.bfloat16)
    tail = jnp.asarray(query_tail(), jnp.float32)
    masks = jnp.asarray(mask_rows(), jnp.float32)
    lanes = jnp.asarray(head_lanes(), jnp.float32)
    in_vmem = pl.BlockSpec(memory_space=pltpu.VMEM)
    in_smem = pl.BlockSpec(memory_space=pltpu.SMEM)
    anywhere = pl.BlockSpec(memory_space=pl.ANY)
    rows = pl.pallas_call(
        kernel,
        out_shape=jax.ShapeDtypeStruct((ROWS, Z, COLS * C), jnp.bfloat16),
        in_specs=[anywhere, in_smem, in_smem]
        + [in_vmem] * 3
        + [anywhere]
        + [in_vmem] * 4
        + [anywhere] * 4,
        out_specs=in_vmem,
        scratch_shapes=[
            pltpu.VMEM((ROWS, Z, COLS * C), jnp.bfloat16),
            pltpu.VMEM((8, C), jnp.float32),
            pltpu.VMEM((2, 1104, 128), jnp.float32),
            pltpu.VMEM((4, 128, 384), jnp.bfloat16),
            pltpu.VMEM((3, 64, 128), jnp.float32),
            pltpu.VMEM((2, 48, 384), jnp.bfloat16),
            pltpu.VMEM((2, 6, 256, 256), jnp.bfloat16),
            pltpu.VMEM((2, C, 3 * C), jnp.bfloat16),
            pltpu.VMEM((2, C, HEADS * 128), jnp.bfloat16),
            pltpu.VMEM((2, C, C), jnp.bfloat16),
            pltpu.VMEM((2, C, 256), jnp.bfloat16),
            pltpu.VMEM((2, C, C), jnp.bfloat16),
            pltpu.VMEM((2, C, 4 * C), jnp.bfloat16),
            pltpu.VMEM((2, 4 * C, C), jnp.bfloat16),
            pltpu.VMEM((2, 2, 4, 2, 48, 384), jnp.bfloat16),
            pltpu.VMEM((TABLES, WW, 16, 256), jnp.bfloat16),
            pltpu.VMEM((2, TOKENS, 128), jnp.float32),
            pltpu.VMEM((2, TOKENS, 128), jnp.float32),
            pltpu.VMEM((STRIPS, 2, CELL, C), jnp.bfloat16),
            pltpu.VMEM((5, CELL, C), jnp.bfloat16),
            pltpu.VMEM((STRIPS, 2, CELL, C), jnp.bfloat16),
            pltpu.VMEM((5, CELL, C), jnp.bfloat16),
            pltpu.SemaphoreType.DMA((6,)),
            pltpu.SemaphoreType.DMA((2, 8)),
            pltpu.SemaphoreType.DMA((2, 8)),
            pltpu.SemaphoreType.DMA((9,)),
            pltpu.SemaphoreType.DMA((9,)),
        ],
        compiler_params=pltpu.CompilerParams(
            collective_id=0, has_side_effects=True, vmem_limit_bytes=56 * 1024 * 1024
        ),
    )(
        tokens.transpose(1, 0, 2),
        surface_ids,
        type_index,
        surface_embed,
        bias_plain.reshape(SHARD_LINES, 128),
        bias_shift.reshape(SHARD_LINES, 128),
        spread,
        tail,
        masks,
        lanes,
        jnp.asarray(head_spread(), jnp.bfloat16),
        w_qkv.reshape(2, C, 3 * C),
        w_proj.reshape(2, C, C),
        w_up,
        w_down.reshape(2, 4 * C, C),
    )
    return rows.transpose(1, 0, 2)


def solution(mesh):
    return jax.shard_map(
        body,
        mesh=mesh,
        in_specs=(
            P(None, "lat", "lon"),
            P("lat", "lon"),
            P(),
            P("lat"),
            P("lon"),
            P("lon"),
            P(),
            P(),
            P(),
            P(),
        ),
        out_specs=P(None, "lat", "lon"),
        check_vma=False,
    )
```

```python
import jax
import jax.numpy as jnp
import numpy as np
from jax import lax
from jax.experimental import pallas as pl
from jax.experimental.pallas import tpu as pltpu
from jax.sharding import PartitionSpec as P

HEADS = 6
HEAD_DIM = 32
C = 192
Z = 8
WZ = 2
WH = 6
WW = 12
ROWS = 12
COLS = 12
RELPOS = 3312
TYPES = 16
SPAN = 2 * WW - 1
STRIPS = 4
CELL = 144
TOKENS = 1152
HALF = 72
TABLES = 48
SHARD_LINES = 621
STRIDE = 69
CHUNKS = 18
KAPPA = WH * SPAN
LON = 16
BIG = 1e30
SCALE = HEAD_DIM**-0.5
PAIR = 2


def slot_positions():
    pos = np.arange(HALF)
    bh, ch, b3, c6 = pos // 36, pos // 18 % 2, pos // 6 % 3, pos % 6
    return bh * 3 + b3, ch * 6 + c6


def spread_matrix():
    b, c = slot_positions()
    out = np.zeros((2, 256, WW, 128), np.float32)
    for lane_type in range(2):
        for query_col in range(WW):
            row = b * SPAN + query_col - c + WW - 1 + lane_type * (KAPPA - 128)
            out[lane_type, row, query_col, np.arange(HALF)] = 1.0
    return out.reshape(2, 256, 6, 256).transpose(0, 2, 1, 3)


def query_tail():
    b, c = slot_positions()
    out = np.zeros((CELL, 256), np.float32)
    for a in range(2):
        rows = a * HALF + np.arange(HALF)
        out[rows, 32 + 16 * c + 8 * a + b] = 1.0
        out[rows, 224] = 1.0
        out[rows, 225 + a] = 1.0
        out[rows, 227 + b // 3] = 1.0
    return out


def mask_rows():
    b, _ = slot_positions()
    out = np.zeros((3, 32, 256), np.float32)
    for a in range(2):
        lanes = a * 128 + np.arange(HALF)
        out[0, 0, a * 128 + HALF : a * 128 + 128] = -BIG
        out[1, 1 + (1 - a), lanes] = -BIG
        out[2, 3 + (1 - b // 3), lanes] = -BIG
    return out


def head_lanes():
    out = np.zeros((HEADS + 1, 1, 256), np.float32)
    for head in range(HEADS):
        out[head, 0, head * HEAD_DIM : (head + 1) * HEAD_DIM] = 1.0
        out[head, 0, C + head] = 1.0
        out[HEADS, 0, C + head] = 1.0
    return out


def head_spread():
    out = np.zeros((256, C), np.float32)
    for head in range(HEADS):
        for row in (64 + head, 192 + head):
            out[row, head * HEAD_DIM : (head + 1) * HEAD_DIM] = 1.0
    return out


def normalised(x):
    center = jnp.sum(x, axis=-1, keepdims=True) * (1.0 / C)
    moved = x - center
    spread = jnp.sum(moved * moved, axis=-1, keepdims=True) * (1.0 / C)
    return moved * lax.rsqrt(spread + 1e-05)


def rounded(x):
    return x.astype(jnp.bfloat16).astype(jnp.float32)


def gelu(v):
    v = v.astype(jnp.bfloat16)
    first, third = jnp.bfloat16(0.7978845608028654), jnp.bfloat16(0.7978845608028654 * 0.044715)
    grown = jnp.tanh(v * (first + third * (v * v)))
    half = jnp.bfloat16(0.5) * v
    return half + half * grown


def dot(a, b):
    return jnp.dot(a, b, preferred_element_type=jnp.float32)


def dot_nt(a, b):
    return lax.dot_general(a, b, (((1,), (1,)), ((), ())), preferred_element_type=jnp.float32)


def take_strided(ref, start):
    near = ref[0, pl.ds(start, HALF, stride=8), :]
    far = ref[1, pl.ds(start, HALF, stride=8), :]
    return jnp.concatenate([near, far[:, : C - 128]], axis=1)


def put_strided(ref, start, value):
    blank = jnp.zeros((HALF, 256 - C), jnp.float32)
    ref[0, pl.ds(start, HALF, stride=8), :] = value[:, :128]
    ref[1, pl.ds(start, HALF, stride=8), :] = jnp.concatenate([value[:, 128:], blank], axis=1)


def take_rows(ref, start, count):
    return jnp.concatenate(
        [ref[0, pl.ds(start, count), :], ref[1, pl.ds(start, count), : C - 128]], axis=1
    )


def put_rows(ref, start, value):
    rows = pl.ds(start, value.shape[0])
    ref[0, rows, :] = value[:, :128]
    ref[1, rows, : C - 128] = value[:, 128:]


def pick_types(block, lines, types, choose, ordered, picked):
    lane = lax.broadcasted_iota(jnp.int32, (1, 384), 1)
    second = lane >= KAPPA
    kappa = jnp.where(second, lane - KAPPA, lane)
    for phase in range(4):
        group = jnp.where(lane < 2 * KAPPA, (kappa + 2 * phase) // 8, -1)
        left = jnp.concatenate(
            [
                lines[block, pl.ds(17 * phase + chunk, 16, stride=STRIDE), :]
                for chunk in range(CHUNKS)
            ],
            axis=0,
        ).astype(jnp.bfloat16)
        wide = dot(left, choose[phase])
        total = jnp.zeros((16, 384), jnp.float32)
        for chunk in range(CHUNKS):
            total = jnp.where(group == chunk, wide[16 * chunk : 16 * chunk + 16], total)
        for tile in range(3):
            ordered[tile, pl.ds(phase, 16, stride=4), :] = total[:, 128 * tile : 128 * tile + 128]
    row = lax.broadcasted_iota(jnp.int32, (8, 384), 0)
    groups = []
    for group in range(6):
        whole = jnp.concatenate([ordered[tile, 6 * group : 6 * group + 8, :] for tile in range(3)], axis=1)
        groups.append(jnp.where(row < 6, whole, 0.0))
    picked[block] = jnp.concatenate(groups, axis=0).astype(jnp.bfloat16)


def choose_lanes(types, choose):
    lane = lax.broadcasted_iota(jnp.int32, (1, 384), 1)
    second = lane >= KAPPA
    kappa = jnp.where(second, lane - KAPPA, lane)
    wanted = jnp.where(second, types[1], types[0])
    row = lax.broadcasted_iota(jnp.int32, (128, 384), 0)
    for phase in range(4):
        target = lax.rem(kappa + 2 * phase, 8) * TYPES + wanted
        target = jnp.where(lane < 2 * KAPPA, target, -1)
        choose[phase] = (row == target).astype(jnp.float32).astype(jnp.bfloat16)


def to_lines(flat, lines):
    count = flat.shape[1] // 128

    def step(at, carry):
        start = pl.multiple_of(at * 2048, 2048)
        chunk = flat[:, pl.ds(start, 2048)].astype(jnp.float32)
        for j in range(16):
            for block in range(2):
                lines[block, pl.ds(at * 16 + j, 1), :] = chunk[
                    block : block + 1, 128 * j : 128 * j + 128
                ]
        return carry

    lax.fori_loop(0, count // 16, step, 0)


def to_matrix(lines, wide, block, rows, columns):
    period = 2 * columns // 128
    parts = [lines[block, pl.ds(j, rows // 2, stride=period), :] for j in range(period)]
    middle = period // 2
    full = columns // 128
    for tile in range(full):
        wide[tile, pl.ds(0, rows // 2, stride=2), :] = parts[tile]
        wide[tile, pl.ds(1, rows // 2, stride=2), :] = jnp.concatenate(
            [parts[middle + tile][:, 64:], parts[middle + tile + 1][:, :64]], axis=1
        )
    wide[full, pl.ds(0, rows // 2, stride=2), :] = parts[middle]
    last = parts[period - 1]
    wide[full, pl.ds(1, rows // 2, stride=2), :] = jnp.concatenate([last[:, 64:], last[:, :64]], axis=1)
    pieces = [wide[tile, 0:rows, :] for tile in range(full)] + [wide[full, 0:rows, 0:64]]
    return jnp.concatenate(pieces, axis=1).astype(jnp.bfloat16)


def prepare_weights(lines, wide, w_q, w_kt, w_v):
    lane = lax.broadcasted_iota(jnp.int32, (1, HEADS * 128), 1)
    inner = lax.rem(lane, 128)
    target = jnp.where(inner < HEAD_DIM, (lane // 128) * HEAD_DIM + inner, -1)
    row = lax.broadcasted_iota(jnp.int32, (C, HEADS * 128), 0)
    place = (row == target).astype(jnp.float32).astype(jnp.bfloat16)
    one = lax.broadcasted_iota(jnp.int32, (C, C), 0) == lax.broadcasted_iota(jnp.int32, (C, C), 1)
    one = one.astype(jnp.float32).astype(jnp.bfloat16)
    for block in range(2):
        qkv = to_matrix(lines, wide, block, C, 3 * C)
        w_q[block] = dot(qkv[:, 0:C], place).astype(jnp.bfloat16)
        w_kt[block] = dot_nt(one, qkv[:, C : 2 * C]).astype(jnp.bfloat16)
        blank = jnp.zeros((C, 256 - C), jnp.bfloat16)
        w_v[block] = jnp.concatenate([qkv[:, 2 * C : 3 * C], blank], axis=1)


def spread_tables(block, gathered, spread, tables):
    for lane_type in range(2):
        lanes = slice(128 * lane_type, 128 * lane_type + 256)
        left = jnp.concatenate(
            [
                gathered[block, c, x_of, z_of, :, lanes]
                for z_of in range(2)
                for x_of in range(4)
                for c in range(2)
            ],
            axis=0,
        )

        def step(pair, carry):
            wide = dot(left, spread[lane_type, pair])
            wide = wide.reshape(24, 2, 2, 8, 256)
            for inner in range(2):
                for a in range(2):
                    part = wide[:, :, a, :, 128 * inner : 128 * inner + 128]
                    part = part.reshape(24, 16, 128).astype(jnp.bfloat16)
                    tables[
                        24 * lane_type : 24 * lane_type + 24,
                        2 * pair + inner,
                        :,
                        128 * a : 128 * a + 128,
                    ] = part
            return carry

        lax.fori_loop(0, 6, step, 0)


def run_windows(block, lat_window, pair, x, y, tables, consts, weights, band):
    tail, masks, lanes, across_heads = consts
    w_q, w_kt, w_v, w_proj, w_up, w_down = weights
    last_band = (band == lax.axis_size("lat") - 1).astype(jnp.float32)
    shifted = block.astype(jnp.float32)
    starts, level_windows = [], []
    for i in range(PAIR):
        level_window = pair * PAIR + i
        level_windows.append(level_window)
        for a in range(2):
            level = lax.rem(2 * level_window + a + block, Z)
            starts.append(lat_window * (HALF * Z) + level)
    parts = [take_strided(x, s) for s in starts]
    stream = jnp.concatenate(parts, axis=0)
    normed = normalised(stream)
    normed_b = normed.astype(jnp.bfloat16)
    queries = dot(normed_b, w_q[block]) * SCALE
    blank = jnp.zeros((128 - HALF, C), jnp.float32)
    mixed_all = []
    for i in range(PAIR):
        first = normed[2 * i * HALF : (2 * i + 1) * HALF]
        second = normed[(2 * i + 1) * HALF : (2 * i + 2) * HALF]
        padded = jnp.concatenate([first, blank, second, blank], axis=0).astype(jnp.bfloat16)
        keys = dot_nt(w_kt[block], padded).astype(jnp.bfloat16)
        values = (dot(padded, w_v[block]) + lanes[HEADS]).astype(jnp.bfloat16)
        on_level = (level_windows[i] == 3).astype(jnp.float32) * shifted
        on_lat = (lat_window == 1).astype(jnp.float32) * last_band * shifted
        mask = masks[0] + masks[1] * on_level + masks[2] * on_lat
        mask = mask.astype(jnp.bfloat16)
        weight_parts, value_parts = [], []
        for head in range(HEADS):
            near = queries[i * CELL : (i + 1) * CELL, 128 * head : 128 * head + 128]
            near = (near + tail[:, 0:128]).astype(jnp.bfloat16)
            far = tail[:, 128:256].astype(jnp.bfloat16)
            left = jnp.concatenate([near, far], axis=1)
            table = tables[lat_window * 24 + level_windows[i] * HEADS + head].reshape(192, 256)
            right = jnp.concatenate([keys[32 * head : 32 * head + 32], table, mask], axis=0)
            scores = dot(left, right)
            top = jnp.max(scores, axis=-1, keepdims=True)
            weight_parts.append(jnp.exp((scores - top).astype(jnp.bfloat16)))
            value_parts.append(values * lanes[head].astype(jnp.bfloat16))
        mixed_all.append(
            dot(jnp.concatenate(weight_parts, axis=1), jnp.concatenate(value_parts, axis=0))
        )
    mixed = jnp.concatenate(mixed_all, axis=0)
    totals = mixed[:, 128:256]
    lane = lax.broadcasted_iota(jnp.int32, totals.shape, 1)
    counted = (lane >= C - 128) & (lane < C - 128 + HEADS)
    inverse = jnp.where(counted, 1.0 / totals, 0.0)
    coarse = inverse.astype(jnp.bfloat16)
    fine = (inverse - coarse.astype(jnp.float32)).astype(jnp.bfloat16)
    scale = dot(jnp.concatenate([coarse, fine], axis=1), across_heads[...])
    mixed = (mixed[:, :C] * scale).astype(jnp.bfloat16)
    middle = rounded(stream + dot(mixed, w_proj[block]))
    lifted = gelu(dot(normalised(middle).astype(jnp.bfloat16), w_up[block]))
    result = middle + dot(lifted, w_down[block])
    for j, s in enumerate(starts):
        put_strided(y, s, result[j * HALF : (j + 1) * HALF])


def kernel(
    tokens_hbm,
    ids,
    types,
    embed_in,
    bias_plain,
    bias_shift,
    spread_hbm,
    tail,
    masks,
    lanes,
    across_heads,
    qkv_hbm,
    proj_hbm,
    up_hbm,
    down_hbm,
    out,
    tokens,
    embed,
    lines,
    choose,
    ordered,
    picked,
    spread,
    qkv,
    w_q,
    w_kt,
    w_v,
    w_proj,
    w_up,
    w_down,
    flat_proj,
    flat_down,
    qkv_lines,
    proj_lines,
    down_lines,
    wide,
    gathered,
    tables,
    x,
    y,
    sent,
    received,
    back,
    returned,
    local_sems,
    gather_send,
    gather_recv,
    halo_send,
    halo_recv,
):
    lat, lon = lax.axis_index("lat"), lax.axis_index("lon")
    lats, lons = lax.axis_size("lat"), lax.axis_size("lon")
    consts = (tail, masks, lanes, across_heads)
    weights = (w_q, w_kt, w_v, w_proj, w_up, w_down)
    north, south = lax.rem(lat + lats - 1, lats), lax.rem(lat + 1, lats)
    west, east = lax.rem(lon + lons - 1, lons), lax.rem(lon + 1, lons)

    sources = (tokens_hbm, qkv_hbm, spread_hbm, proj_hbm, up_hbm, down_hbm)
    targets = (tokens, qkv, spread, flat_proj, w_up, flat_down)
    loads = [
        pltpu.make_async_copy(source, target, local_sems.at[i])
        for i, (source, target) in enumerate(zip(sources, targets))
    ]
    for load in loads:
        load.start()

    def place(i, j):
        return {"lat": i, "lon": j}

    crosses, sides = 2, 2
    across = lons // (crosses * sides)
    core, x_at, z_at = lax.rem(lon, sides), lax.rem(lon // sides, across), lon // (sides * across)

    def lon_of(z, x, c):
        return (z * across + x) * sides + c

    opposite = lon_of(1 - z_at, x_at, core)
    sibling = lon_of(z_at, x_at, 1 - core)
    peers = [lon_of(z_at, lax.rem(x_at + step, across), core) for step in range(1, 4)]
    origins = [lax.rem(x_at + across - step, across) for step in range(1, 4)]
    partners = [(lat, j) for j in (opposite, sibling, *peers, west, east)]
    partners += [(north, lon), (south, lon), (north, west), (south, east)]

    barrier = pltpu.get_barrier_semaphore()
    for i, j in partners:
        pl.semaphore_signal(
            barrier, inc=1, device_id=place(i, j), device_id_type=pl.DeviceIdType.MESH
        )

    def share(block, index, source, slot, target):
        return pltpu.make_async_remote_copy(
            src_ref=source,
            dst_ref=slot,
            send_sem=gather_send.at[block, index],
            recv_sem=gather_recv.at[block, index],
            device_id=place(lat, target),
            device_id_type=pl.DeviceIdType.MESH,
        )

    def slot(block, x_of, z_of):
        return gathered.at[block, core, x_of, z_of]

    def own_copy(block, i):
        target = opposite if i == 0 else peers[i - 1]
        return share(block, i, picked.at[block], slot(block, x_at, z_at), target)

    def passed_copy(block, i):
        held = slot(block, x_at, 1 - z_at)
        return share(block, 4 + i, held, held, peers[i])

    def sibling_copy(block):
        held = gathered.at[block, core]
        return share(block, 7, held, held, sibling)

    def wait_opposite(block):
        share(block, 0, picked.at[block], slot(block, x_at, 1 - z_at), opposite).wait_recv()

    def wait_peers(block):
        for i, origin in enumerate(origins):
            share(block, 1 + i, picked.at[block], slot(block, origin, z_at), lon).wait_recv()
        for i, origin in enumerate(origins):
            share(block, 4 + i, picked.at[block], slot(block, origin, 1 - z_at), lon).wait_recv()

    def wait_sibling(block):
        other = gathered.at[block, 1 - core]
        share(block, 7, other, other, sibling).wait_recv()

    lines[0, 0:SHARD_LINES] = bias_plain[...].astype(jnp.float32)
    lines[1, 0:SHARD_LINES] = bias_shift[...].astype(jnp.float32)
    choose_lanes(types, choose)
    pl.semaphore_wait(barrier, len(partners))

    def pick_and_send(block):
        pick_types(block, lines, types, choose, ordered, picked)
        for i in range(4):
            own_copy(block, i).start()
        gathered[block, core, x_at, z_at] = picked[block]

    pick_and_send(0)

    embed[0:3, :] = embed_in[...].astype(jnp.float32)
    loads[0].wait()

    def embed_row(row, carry):
        strip, inner = row // 3, row % 3
        for col in range(COLS):
            cell = tokens[row, :, C * col : C * col + C].astype(jnp.float32)
            line = embed[pl.ds(ids[row, col], 1), :]
            start = ((strip * 2 + col // 6) * 18 + inner * 6 + col % 6) * 8
            put_rows(x, pl.multiple_of(start, 8), rounded(cell + line))
        return carry

    lax.fori_loop(0, ROWS, embed_row, 0)

    def pass_on(block):
        wait_opposite(block)
        for i in range(3):
            passed_copy(block, i).start()

    pass_on(0)
    loads[1].wait()
    to_lines(qkv, qkv_lines)
    prepare_weights(qkv_lines, wide, w_q, w_kt, w_v)
    loads[3].wait()
    to_lines(flat_proj, proj_lines)
    for block in range(2):
        w_proj[block] = to_matrix(proj_lines, wide, block, C, C)
    wait_peers(0)
    sibling_copy(0).start()
    pick_and_send(1)
    loads[5].wait()
    to_lines(flat_down, down_lines)
    for block in range(2):
        w_down[block] = to_matrix(down_lines, wide, block, 4 * C, C)
    loads[2].wait()
    loads[4].wait()

    def halo(index, source, target, i, j):
        return pltpu.make_async_remote_copy(
            src_ref=source,
            dst_ref=target,
            send_sem=halo_send.at[index],
            recv_sem=halo_recv.at[index],
            device_id=place(i, j),
            device_id_type=pl.DeviceIdType.MESH,
        )

    ahead = [
        halo(0, sent.at[0, 0], received.at[4], north, west),
        halo(1, sent.at[0, 1], received.at[3], north, lon),
        halo(2, sent.at[1, 0], received.at[0], lat, west),
        halo(3, sent.at[3, 0], received.at[2], lat, west),
        halo(4, sent.at[2, 0], received.at[1], lat, west),
    ]
    home = [
        halo(5, back.at[3, 1], returned.at[4], south, east),
        halo(6, back.at[3, 0], returned.at[3], south, lon),
        halo(7, back.at[2, 1], returned.at[2], lat, east),
        halo(8, back.at[0:2, 1], returned.at[0:2], lat, east),
    ]

    def narrow(target, strips):
        for strip in strips:
            for half in range(2):
                start = (strip * 2 + half) * CELL
                target[strip, half] = take_rows(y, start, CELL).astype(jnp.bfloat16)

    def widen(strip, half, source):
        put_rows(x, (strip * 2 + half) * CELL, source.astype(jnp.float32))

    def step(at, carry):
        stage, pair = at // 2, lax.rem(at, 2)
        block = stage // 2
        lat_window = jnp.where(block == 0, stage, 3 - stage)

        @pl.when(lax.rem(at, 4) == 0)
        def _():
            wait_sibling(block)
            spread_tables(block, gathered, spread, tables)

        @pl.when(at == 4)
        def _():
            widen(2, 0, sent[3, 1])
            for i in (3, 1, 0):
                ahead[i].wait_recv()
            widen(2, 1, received[2])
            widen(3, 0, received[3])
            widen(3, 1, received[4])

        @pl.when(at == 6)
        def _():
            widen(0, 0, sent[1, 1])
            widen(1, 0, sent[2, 1])
            ahead[2].wait_recv()
            ahead[4].wait_recv()
            widen(0, 1, received[0])
            widen(1, 1, received[1])

        run_windows(block, lat_window, pair, x, y, tables, consts, weights, lat)

        @pl.when(at == 0)
        def _():
            pass_on(1)

        @pl.when(at == 1)
        def _():
            narrow(sent, (0, 1))
            for i in (0, 1, 2):
                ahead[i].start()
            wait_peers(1)
            sibling_copy(1).start()

        @pl.when(at == 3)
        def _():
            narrow(sent, (2, 3))
            for i in (3, 4):
                ahead[i].start()

        @pl.when(at == 5)
        def _():
            narrow(back, (2, 3))
            for i in (0, 1, 2):
                home[i].start()

        @pl.when(at == 7)
        def _():
            narrow(back, (0, 1))
            home[3].start()

        return carry

    lax.fori_loop(0, 8, step, 0)

    def put(strip, half, cells):
        for inner in range(3):
            for col in range(6):
                at = (inner * 6 + col) * 8
                lane = (half * 6 + col) * C
                out[strip * 3 + inner, :, lane : lane + C] = cells[at : at + 8].astype(jnp.bfloat16)

    for strip in range(3):
        put(strip + 1, 1, back[strip, 0].astype(jnp.float32))
    for copy in ahead:
        copy.wait_send()
    for block in range(2):
        for i in range(4):
            own_copy(block, i).wait_send()
        for i in range(3):
            passed_copy(block, i).wait_send()
        sibling_copy(block).wait_send()
    for copy in home[:3]:
        copy.wait()
    put(3, 0, returned[2].astype(jnp.float32))
    put(0, 1, returned[3].astype(jnp.float32))
    put(0, 0, returned[4].astype(jnp.float32))
    home[3].wait()
    for strip in range(2):
        put(strip + 1, 0, returned[strip].astype(jnp.float32))


def body(
    tokens,
    surface_ids,
    surface_embed,
    type_index,
    bias_plain,
    bias_shift,
    w_qkv,
    w_proj,
    w_up,
    w_down,
):
    spread = jnp.asarray(spread_matrix(), jnp.bfloat16)
    tail = jnp.asarray(query_tail(), jnp.float32)
    masks = jnp.asarray(mask_rows(), jnp.float32)
    lanes = jnp.asarray(head_lanes(), jnp.float32)
    in_vmem = pl.BlockSpec(memory_space=pltpu.VMEM)
    in_smem = pl.BlockSpec(memory_space=pltpu.SMEM)
    anywhere = pl.BlockSpec(memory_space=pl.ANY)
    rows = pl.pallas_call(
        kernel,
        out_shape=jax.ShapeDtypeStruct((ROWS, Z, COLS * C), jnp.bfloat16),
        in_specs=[anywhere, in_smem, in_smem]
        + [in_vmem] * 3
        + [anywhere]
        + [in_vmem] * 4
        + [anywhere] * 4,
        out_specs=in_vmem,
        scratch_shapes=[
            pltpu.VMEM((ROWS, Z, COLS * C), jnp.bfloat16),
            pltpu.VMEM((8, C), jnp.float32),
            pltpu.VMEM((2, 1104, 128), jnp.float32),
            pltpu.VMEM((4, 128, 384), jnp.bfloat16),
            pltpu.VMEM((3, 64, 128), jnp.float32),
            pltpu.VMEM((2, 48, 384), jnp.bfloat16),
            pltpu.VMEM((2, 6, 256, 256), jnp.bfloat16),
            pltpu.VMEM((2, 3 * C * C), jnp.bfloat16),
            pltpu.VMEM((2, C, HEADS * 128), jnp.bfloat16),
            pltpu.VMEM((2, C, C), jnp.bfloat16),
            pltpu.VMEM((2, C, 256), jnp.bfloat16),
            pltpu.VMEM((2, C, C), jnp.bfloat16),
            pltpu.VMEM((2, C, 4 * C), jnp.bfloat16),
            pltpu.VMEM((2, 4 * C, C), jnp.bfloat16),
            pltpu.VMEM((2, C * C), jnp.bfloat16),
            pltpu.VMEM((2, 4 * C * C), jnp.bfloat16),
            pltpu.VMEM((2, 3 * C * C // 128, 128), jnp.float32),
            pltpu.VMEM((2, C * C // 128, 128), jnp.float32),
            pltpu.VMEM((2, 4 * C * C // 128, 128), jnp.float32),
            pltpu.VMEM((5, 4 * C, 128), jnp.float32),
            pltpu.VMEM((2, 2, 4, 2, 48, 384), jnp.bfloat16),
            pltpu.VMEM((TABLES, WW, 16, 256), jnp.bfloat16),
            pltpu.VMEM((2, TOKENS, 128), jnp.float32),
            pltpu.VMEM((2, TOKENS, 128), jnp.float32),
            pltpu.VMEM((STRIPS, 2, CELL, C), jnp.bfloat16),
            pltpu.VMEM((5, CELL, C), jnp.bfloat16),
            pltpu.VMEM((STRIPS, 2, CELL, C), jnp.bfloat16),
            pltpu.VMEM((5, CELL, C), jnp.bfloat16),
            pltpu.SemaphoreType.DMA((6,)),
            pltpu.SemaphoreType.DMA((2, 8)),
            pltpu.SemaphoreType.DMA((2, 8)),
            pltpu.SemaphoreType.DMA((9,)),
            pltpu.SemaphoreType.DMA((9,)),
        ],
        compiler_params=pltpu.CompilerParams(
            collective_id=0, has_side_effects=True, vmem_limit_bytes=56 * 1024 * 1024
        ),
    )(
        tokens.transpose(1, 0, 2),
        surface_ids,
        type_index,
        surface_embed,
        bias_plain.reshape(SHARD_LINES, 128),
        bias_shift.reshape(SHARD_LINES, 128),
        spread,
        tail,
        masks,
        lanes,
        jnp.asarray(head_spread(), jnp.bfloat16),
        w_qkv,
        w_proj,
        w_up,
        w_down,
    )
    return rows.transpose(1, 0, 2)


def solution(mesh):
    return jax.shard_map(
        body,
        mesh=mesh,
        in_specs=(
            P(None, "lat", "lon"),
            P("lat", "lon"),
            P(),
            P("lat"),
            P("lon"),
            P("lon"),
            P(),
            P(),
            P(),
            P(),
        ),
        out_specs=P(None, "lat", "lon"),
        check_vma=False,
    )
```

```python
import jax
import jax.numpy as jnp
import numpy as np
from jax import lax
from jax.experimental import pallas as pl
from jax.experimental.pallas import tpu as pltpu
from jax.sharding import PartitionSpec as P

HEADS = 6
HEAD_DIM = 32
C = 192
Z = 8
WZ = 2
WH = 6
WW = 12
ROWS = 12
COLS = 12
RELPOS = 3312
TYPES = 16
SPAN = 2 * WW - 1
STRIPS = 4
CELL = 144
TOKENS = 1152
HALF = 72
TABLES = 48
SHARD_LINES = 621
STRIDE = 69
CHUNKS = 18
KAPPA = WH * SPAN
LON = 16
BIG = 1e30
SCALE = HEAD_DIM**-0.5
PAIR = 2


def slot_positions():
    pos = np.arange(HALF)
    bh, ch, b3, c6 = pos // 36, pos // 18 % 2, pos // 6 % 3, pos % 6
    return bh * 3 + b3, ch * 6 + c6


def spread_matrix():
    b, c = slot_positions()
    out = np.zeros((2, 256, WW, 128), np.float32)
    for lane_type in range(2):
        for query_col in range(WW):
            row = b * SPAN + query_col - c + WW - 1 + lane_type * (KAPPA - 128)
            out[lane_type, row, query_col, np.arange(HALF)] = 1.0
    return out.reshape(2, 256, 6, 256).transpose(0, 2, 1, 3)


def query_tail():
    b, c = slot_positions()
    out = np.zeros((CELL, 256), np.float32)
    for a in range(2):
        rows = a * HALF + np.arange(HALF)
        out[rows, 32 + 16 * c + 8 * a + b] = 1.0
        out[rows, 224] = 1.0
        out[rows, 225 + a] = 1.0
        out[rows, 227 + b // 3] = 1.0
    return out


def mask_rows():
    b, _ = slot_positions()
    out = np.zeros((3, 32, 256), np.float32)
    for a in range(2):
        lanes = a * 128 + np.arange(HALF)
        out[0, 0, a * 128 + HALF : a * 128 + 128] = -BIG
        out[1, 1 + (1 - a), lanes] = -BIG
        out[2, 3 + (1 - b // 3), lanes] = -BIG
    return out


def head_lanes():
    out = np.zeros((HEADS + 1, 1, 256), np.float32)
    for head in range(HEADS):
        out[head, 0, head * HEAD_DIM : (head + 1) * HEAD_DIM] = 1.0
        out[head, 0, C + head] = 1.0
        out[HEADS, 0, C + head] = 1.0
    return out


def head_spread():
    out = np.zeros((256, C), np.float32)
    for head in range(HEADS):
        for row in (64 + head, 192 + head):
            out[row, head * HEAD_DIM : (head + 1) * HEAD_DIM] = 1.0
    return out


def normalised(x):
    center = jnp.sum(x, axis=-1, keepdims=True) * (1.0 / C)
    moved = x - center
    spread = jnp.sum(moved * moved, axis=-1, keepdims=True) * (1.0 / C)
    return moved * lax.rsqrt(spread + 1e-05)


def rounded(x):
    return x.astype(jnp.bfloat16).astype(jnp.float32)


def gelu(v):
    v = v.astype(jnp.bfloat16)
    first, third = jnp.bfloat16(0.7978845608028654), jnp.bfloat16(0.7978845608028654 * 0.044715)
    grown = jnp.tanh(v * (first + third * (v * v)))
    half = jnp.bfloat16(0.5) * v
    return half + half * grown


def dot(a, b):
    return jnp.dot(a, b, preferred_element_type=jnp.float32)


def dot_nt(a, b):
    return lax.dot_general(a, b, (((1,), (1,)), ((), ())), preferred_element_type=jnp.float32)


def row_of(level, lat_window):
    return (level // 4) * (TOKENS // 2) + lat_window * (HALF * 4) + lax.rem(level, 4)


def take_strided(ref, start):
    near = ref[0, pl.ds(start, HALF, stride=4), :]
    far = ref[1, pl.ds(start, HALF, stride=4), :]
    return jnp.concatenate([near, far[:, : C - 128]], axis=1)


def put_strided(ref, start, value):
    blank = jnp.zeros((HALF, 256 - C), jnp.float32)
    ref[0, pl.ds(start, HALF, stride=4), :] = value[:, :128]
    ref[1, pl.ds(start, HALF, stride=4), :] = jnp.concatenate([value[:, 128:], blank], axis=1)


def take_rows(ref, start, count):
    return jnp.concatenate(
        [ref[0, pl.ds(start, count), :], ref[1, pl.ds(start, count), : C - 128]], axis=1
    )


def put_rows(ref, start, value):
    rows = pl.ds(start, value.shape[0])
    ref[0, rows, :] = value[:, :128]
    ref[1, rows, : C - 128] = value[:, 128:]


def pick_types(block, lines, types, choose, ordered, picked):
    lane = lax.broadcasted_iota(jnp.int32, (1, 384), 1)
    second = lane >= KAPPA
    kappa = jnp.where(second, lane - KAPPA, lane)
    for phase in range(4):
        group = jnp.where(lane < 2 * KAPPA, (kappa + 2 * phase) // 8, -1)
        left = jnp.concatenate(
            [
                lines[block, pl.ds(17 * phase + chunk, 16, stride=STRIDE), :]
                for chunk in range(CHUNKS)
            ],
            axis=0,
        ).astype(jnp.bfloat16)
        wide = dot(left, choose[phase])
        total = jnp.zeros((16, 384), jnp.float32)
        for chunk in range(CHUNKS):
            total = jnp.where(group == chunk, wide[16 * chunk : 16 * chunk + 16], total)
        for tile in range(3):
            ordered[tile, pl.ds(phase, 16, stride=4), :] = total[:, 128 * tile : 128 * tile + 128]
    row = lax.broadcasted_iota(jnp.int32, (8, 384), 0)
    groups = []
    for group in range(6):
        whole = jnp.concatenate([ordered[tile, 6 * group : 6 * group + 8, :] for tile in range(3)], axis=1)
        groups.append(jnp.where(row < 6, whole, 0.0))
    picked[block] = jnp.concatenate(groups, axis=0).astype(jnp.bfloat16)


def choose_lanes(types, choose):
    lane = lax.broadcasted_iota(jnp.int32, (1, 384), 1)
    second = lane >= KAPPA
    kappa = jnp.where(second, lane - KAPPA, lane)
    wanted = jnp.where(second, types[1], types[0])
    row = lax.broadcasted_iota(jnp.int32, (128, 384), 0)
    for phase in range(4):
        target = lax.rem(kappa + 2 * phase, 8) * TYPES + wanted
        target = jnp.where(lane < 2 * KAPPA, target, -1)
        choose[phase] = (row == target).astype(jnp.float32).astype(jnp.bfloat16)


def to_lines(flat, lines):
    count = flat.shape[1] // 128

    def step(at, carry):
        start = pl.multiple_of(at * 2048, 2048)
        chunk = flat[:, pl.ds(start, 2048)].astype(jnp.float32)
        for j in range(16):
            for block in range(2):
                lines[block, pl.ds(at * 16 + j, 1), :] = chunk[
                    block : block + 1, 128 * j : 128 * j + 128
                ]
        return carry

    lax.fori_loop(0, count // 16, step, 0)


def to_matrix(lines, wide, block, rows, columns):
    period = 2 * columns // 128
    parts = [lines[block, pl.ds(j, rows // 2, stride=period), :] for j in range(period)]
    middle = period // 2
    full = columns // 128
    for tile in range(full):
        wide[tile, pl.ds(0, rows // 2, stride=2), :] = parts[tile]
        wide[tile, pl.ds(1, rows // 2, stride=2), :] = jnp.concatenate(
            [parts[middle + tile][:, 64:], parts[middle + tile + 1][:, :64]], axis=1
        )
    wide[full, pl.ds(0, rows // 2, stride=2), :] = parts[middle]
    last = parts[period - 1]
    wide[full, pl.ds(1, rows // 2, stride=2), :] = jnp.concatenate([last[:, 64:], last[:, :64]], axis=1)
    pieces = [wide[tile, 0:rows, :] for tile in range(full)] + [wide[full, 0:rows, 0:64]]
    return jnp.concatenate(pieces, axis=1).astype(jnp.bfloat16)


def prepare_weights(lines, wide, w_q, w_kt, w_v):
    lane = lax.broadcasted_iota(jnp.int32, (1, HEADS * 128), 1)
    inner = lax.rem(lane, 128)
    target = jnp.where(inner < HEAD_DIM, (lane // 128) * HEAD_DIM + inner, -1)
    row = lax.broadcasted_iota(jnp.int32, (C, HEADS * 128), 0)
    place = (row == target).astype(jnp.float32).astype(jnp.bfloat16)
    one = lax.broadcasted_iota(jnp.int32, (C, C), 0) == lax.broadcasted_iota(jnp.int32, (C, C), 1)
    one = one.astype(jnp.float32).astype(jnp.bfloat16)
    for block in range(2):
        qkv = to_matrix(lines, wide, block, C, 3 * C)
        w_q[block] = dot(qkv[:, 0:C], place).astype(jnp.bfloat16)
        w_kt[block] = dot_nt(one, qkv[:, C : 2 * C]).astype(jnp.bfloat16)
        blank = jnp.zeros((C, 256 - C), jnp.bfloat16)
        w_v[block] = jnp.concatenate([qkv[:, 2 * C : 3 * C], blank], axis=1)


def spread_tables(block, gathered, spread, tables):
    for lane_type in range(2):
        lanes = slice(128 * lane_type, 128 * lane_type + 256)
        left = jnp.concatenate(
            [
                gathered[block, c, x_of, z_of, :, lanes]
                for z_of in range(2)
                for x_of in range(4)
                for c in range(2)
            ],
            axis=0,
        )

        def step(pair, carry):
            wide = dot(left, spread[lane_type, pair])
            wide = wide.reshape(24, 2, 2, 8, 256)
            for inner in range(2):
                for a in range(2):
                    part = wide[:, :, a, :, 128 * inner : 128 * inner + 128]
                    part = part.reshape(24, 16, 128).astype(jnp.bfloat16)
                    tables[
                        24 * lane_type : 24 * lane_type + 24,
                        2 * pair + inner,
                        :,
                        128 * a : 128 * a + 128,
                    ] = part
            return carry

        lax.fori_loop(0, 6, step, 0, unroll=3)


def run_windows(block, lat_window, pair, x, y, tables, consts, weights, band):
    tail, masks, lanes, across_heads = consts
    w_q, w_kt, w_v, w_proj, w_up, w_down = weights
    last_band = (band == lax.axis_size("lat") - 1).astype(jnp.float32)
    shifted = block.astype(jnp.float32)
    starts, ends, level_windows = [], [], []
    for i in range(PAIR):
        level_window = pair * PAIR + i
        level_windows.append(level_window)
        for a in range(2):
            rolled = 2 * level_window + a
            level = lax.rem(rolled + block, Z)
            starts.append(row_of(level, lat_window))
            ends.append(row_of(rolled, lat_window))
    parts = [take_strided(x, s) for s in starts]
    stream = jnp.concatenate(parts, axis=0)
    normed = normalised(stream)
    normed_b = normed.astype(jnp.bfloat16)
    queries = dot(normed_b, w_q[block]) * SCALE
    blank = jnp.zeros((128 - HALF, C), jnp.float32)
    mixed_all = []
    for i in range(PAIR):
        first = normed[2 * i * HALF : (2 * i + 1) * HALF]
        second = normed[(2 * i + 1) * HALF : (2 * i + 2) * HALF]
        padded = jnp.concatenate([first, blank, second, blank], axis=0).astype(jnp.bfloat16)
        keys = dot_nt(w_kt[block], padded).astype(jnp.bfloat16)
        values = (dot(padded, w_v[block]) + lanes[HEADS]).astype(jnp.bfloat16)
        on_level = (level_windows[i] == 3).astype(jnp.float32) * shifted
        on_lat = (lat_window == 1).astype(jnp.float32) * last_band * shifted
        mask = masks[0] + masks[1] * on_level + masks[2] * on_lat
        mask = mask.astype(jnp.bfloat16)
        weight_parts, value_parts = [], []
        for head in range(HEADS):
            near = queries[i * CELL : (i + 1) * CELL, 128 * head : 128 * head + 128]
            near = (near + tail[:, 0:128]).astype(jnp.bfloat16)
            far = tail[:, 128:256].astype(jnp.bfloat16)
            left = jnp.concatenate([near, far], axis=1)
            table = tables[lat_window * 24 + level_windows[i] * HEADS + head].reshape(192, 256)
            right = jnp.concatenate([keys[32 * head : 32 * head + 32], table, mask], axis=0)
            scores = dot(left, right)
            top = jnp.max(scores, axis=-1, keepdims=True)
            weight_parts.append(jnp.exp((scores - top).astype(jnp.bfloat16)))
            value_parts.append(values * lanes[head].astype(jnp.bfloat16))
        mixed_all.append(
            dot(jnp.concatenate(weight_parts, axis=1), jnp.concatenate(value_parts, axis=0))
        )
    mixed = jnp.concatenate(mixed_all, axis=0)
    totals = mixed[:, 128:256]
    lane = lax.broadcasted_iota(jnp.int32, totals.shape, 1)
    counted = (lane >= C - 128) & (lane < C - 128 + HEADS)
    inverse = jnp.where(counted, 1.0 / totals, 0.0)
    coarse = inverse.astype(jnp.bfloat16)
    fine = (inverse - coarse.astype(jnp.float32)).astype(jnp.bfloat16)
    scale = dot(jnp.concatenate([coarse, fine], axis=1), across_heads[...])
    mixed = (mixed[:, :C] * scale).astype(jnp.bfloat16)
    middle = rounded(stream + dot(mixed, w_proj[block]))
    lifted = gelu(dot(normalised(middle).astype(jnp.bfloat16), w_up[block]))
    result = middle + dot(lifted, w_down[block])
    for j, s in enumerate(ends):
        put_strided(y, s, result[j * HALF : (j + 1) * HALF])


def kernel(
    tokens_hbm,
    ids,
    types,
    embed_in,
    bias_plain,
    bias_shift,
    spread_hbm,
    tail,
    masks,
    lanes,
    across_heads,
    qkv_hbm,
    proj_hbm,
    up_hbm,
    down_hbm,
    out,
    tokens,
    embed,
    lines,
    choose,
    ordered,
    picked,
    spread,
    qkv,
    w_q,
    w_kt,
    w_v,
    w_proj,
    w_up,
    w_down,
    flat_proj,
    flat_down,
    qkv_lines,
    proj_lines,
    down_lines,
    wide,
    gathered,
    tables,
    x,
    y,
    moved,
    received,
    returned,
    local_sems,
    gather_send,
    gather_recv,
    halo_send,
    halo_recv,
):
    lat, lon = lax.axis_index("lat"), lax.axis_index("lon")
    lats, lons = lax.axis_size("lat"), lax.axis_size("lon")
    consts = (tail, masks, lanes, across_heads)
    weights = (w_q, w_kt, w_v, w_proj, w_up, w_down)
    north, south = lax.rem(lat + lats - 1, lats), lax.rem(lat + 1, lats)
    west, east = lax.rem(lon + lons - 1, lons), lax.rem(lon + 1, lons)

    sources = (tokens_hbm, qkv_hbm, spread_hbm, proj_hbm, up_hbm, down_hbm)
    targets = (tokens, qkv, spread, flat_proj, w_up, flat_down)
    loads = [
        pltpu.make_async_copy(source, target, local_sems.at[i])
        for i, (source, target) in enumerate(zip(sources, targets))
    ]
    for load in loads:
        load.start()

    def place(i, j):
        return {"lat": i, "lon": j}

    crosses, sides = 2, 2
    across = lons // (crosses * sides)
    core, x_at, z_at = lax.rem(lon, sides), lax.rem(lon // sides, across), lon // (sides * across)

    def lon_of(z, x, c):
        return (z * across + x) * sides + c

    opposite = lon_of(1 - z_at, x_at, core)
    sibling = lon_of(z_at, x_at, 1 - core)
    peers = [lon_of(z_at, lax.rem(x_at + step, across), core) for step in range(1, 4)]
    origins = [lax.rem(x_at + across - step, across) for step in range(1, 4)]
    partners = [(lat, j) for j in (opposite, sibling, *peers, west, east)]
    partners += [(north, lon), (south, lon), (north, west), (south, east)]

    barrier = pltpu.get_barrier_semaphore()
    for i, j in partners:
        pl.semaphore_signal(
            barrier, inc=1, device_id=place(i, j), device_id_type=pl.DeviceIdType.MESH
        )

    def share(block, index, source, slot, target):
        return pltpu.make_async_remote_copy(
            src_ref=source,
            dst_ref=slot,
            send_sem=gather_send.at[block, index],
            recv_sem=gather_recv.at[block, index],
            device_id=place(lat, target),
            device_id_type=pl.DeviceIdType.MESH,
        )

    def slot(block, x_of, z_of):
        return gathered.at[block, core, x_of, z_of]

    def own_copy(block, i):
        target = opposite if i == 0 else peers[i - 1]
        return share(block, i, picked.at[block], slot(block, x_at, z_at), target)

    def passed_copy(block, i):
        held = slot(block, x_at, 1 - z_at)
        return share(block, 4 + i, held, held, peers[i])

    def sibling_copy(block):
        held = gathered.at[block, core]
        return share(block, 7, held, held, sibling)

    def wait_opposite(block):
        share(block, 0, picked.at[block], slot(block, x_at, 1 - z_at), opposite).wait_recv()

    def wait_peers(block):
        for i, origin in enumerate(origins):
            share(block, 1 + i, picked.at[block], slot(block, origin, z_at), lon).wait_recv()
        for i, origin in enumerate(origins):
            share(block, 4 + i, picked.at[block], slot(block, origin, 1 - z_at), lon).wait_recv()

    def wait_sibling(block):
        other = gathered.at[block, 1 - core]
        share(block, 7, other, other, sibling).wait_recv()

    lines[0, 0:SHARD_LINES] = bias_plain[...].astype(jnp.float32)
    lines[1, 0:SHARD_LINES] = bias_shift[...].astype(jnp.float32)
    choose_lanes(types, choose)
    pl.semaphore_wait(barrier, len(partners))

    def pick_and_send(block):
        pick_types(block, lines, types, choose, ordered, picked)
        for i in range(4):
            own_copy(block, i).start()
        gathered[block, core, x_at, z_at] = picked[block]

    pick_and_send(0)

    embed[0:3, :] = embed_in[...].astype(jnp.float32)
    loads[0].wait()

    def embed_row(row, carry):
        strip, inner = row // 3, row % 3
        for col in range(0, COLS, 2):
            cells = []
            for c in (col, col + 1):
                cell = tokens[row, :, C * c : C * c + C].astype(jnp.float32)
                cells.append(rounded(cell + embed[pl.ds(ids[row, c], 1), :]))
            for part in range(2):
                start = part * (TOKENS // 2) + (strip * 2 + col // 6) * HALF
                start = pl.multiple_of(start + (inner * 6 + col % 6) * 4, 8)
                rows = [cell[4 * part : 4 * part + 4] for cell in cells]
                put_rows(x, start, jnp.concatenate(rows, axis=0))
        return carry

    lax.fori_loop(0, ROWS, embed_row, 0)

    def pass_on(block):
        wait_opposite(block)
        for i in range(3):
            passed_copy(block, i).start()

    pass_on(0)
    loads[1].wait()
    to_lines(qkv, qkv_lines)
    prepare_weights(qkv_lines, wide, w_q, w_kt, w_v)
    loads[3].wait()
    to_lines(flat_proj, proj_lines)
    for block in range(2):
        w_proj[block] = to_matrix(proj_lines, wide, block, C, C)
    wait_peers(0)
    sibling_copy(0).start()
    pick_and_send(1)
    loads[5].wait()
    to_lines(flat_down, down_lines)
    for block in range(2):
        w_down[block] = to_matrix(down_lines, wide, block, 4 * C, C)
    loads[2].wait()
    loads[4].wait()

    def halo(index, source, target, i, j):
        return pltpu.make_async_remote_copy(
            src_ref=source,
            dst_ref=target,
            send_sem=halo_send.at[index],
            recv_sem=halo_recv.at[index],
            device_id=place(i, j),
            device_id_type=pl.DeviceIdType.MESH,
        )

    sent, back = moved.at[0], moved.at[1]
    ahead = [
        halo(0, sent.at[:, 0, 0], received.at[:, 4], north, west),
        halo(1, sent.at[:, 1, 0], received.at[:, 3], north, lon),
        halo(2, sent.at[:, 0, 1], received.at[:, 0], lat, west),
    ]
    ahead += [halo(3 + p, sent.at[p, 0, 3], received.at[p, 2], lat, west) for p in range(2)]
    ahead += [halo(5 + p, sent.at[p, 0, 2], received.at[p, 1], lat, west) for p in range(2)]
    home = []
    for p in range(2):
        home += [
            halo(7 + 3 * p, back.at[p, 1, 3], returned.at[p, 4], south, east),
            halo(8 + 3 * p, back.at[p, 0, 3], returned.at[p, 3], south, lon),
            halo(9 + 3 * p, back.at[p, 1, 2], returned.at[p, 2], lat, east),
        ]
    home += [halo(13 + p, back.at[p, 1, 0:2], returned.at[p, 0:2], lat, east) for p in range(2)]

    def piece(p, strip, half):
        return p * (TOKENS // 2) + (strip * 2 + half) * HALF

    def narrow(block, p, lat_window):
        blank = jnp.zeros((80 - HALF, C), jnp.float32)
        for bh in range(2):
            for half in range(2):
                strip = 2 * lat_window + bh
                rows = take_rows(y, pl.multiple_of(piece(p, strip, half), 8), HALF)
                rows = jnp.concatenate([rows, blank], axis=0)
                moved[block, p, half, strip] = rows.astype(jnp.bfloat16)

    def widen(target, p, strip, half, source):
        put_rows(target, piece(p, strip, half), source.astype(jnp.float32)[:HALF])

    def step(at, carry):
        stage, pair = at // 2, lax.rem(at, 2)
        block = stage // 2
        lat_window = jnp.where(block == 0, stage, 3 - stage)

        @pl.when(lax.rem(at, 4) == 0)
        def _():
            wait_sibling(block)
            spread_tables(block, gathered, spread, tables)

        @pl.when(at == 4)
        def _():
            for p in range(2):
                widen(x, p, 2, 0, sent[p, 1, 3])
            for i in (0, 1, 3, 4):
                ahead[i].wait_recv()
            for p in range(2):
                widen(x, p, 2, 1, received[p, 2])
                widen(x, p, 3, 0, received[p, 3])
                widen(x, p, 3, 1, received[p, 4])

        @pl.when(at == 6)
        def _():
            for p in range(2):
                widen(x, p, 0, 0, sent[p, 1, 1])
                widen(x, p, 1, 0, sent[p, 1, 2])
            for i in (2, 5, 6):
                ahead[i].wait_recv()
            for p in range(2):
                widen(x, p, 0, 1, received[p, 0])
                widen(x, p, 1, 1, received[p, 1])

        run_windows(block, lat_window, pair, x, y, tables, consts, weights, lat)

        narrow(block, pair, lat_window)

        def after(when, copies):
            @pl.when(at == when)
            def _():
                for copy in copies:
                    copy.start()

        after(1, ahead[0:3])
        after(2, [ahead[3], ahead[5]])
        after(3, [ahead[4], ahead[6]])
        after(4, home[0:3])
        after(5, home[3:6])
        after(6, home[6:7])
        after(7, home[7:8])

        @pl.when(at == 0)
        def _():
            pass_on(1)

        @pl.when(at == 1)
        def _():
            wait_peers(1)
            sibling_copy(1).start()

        return carry

    lax.fori_loop(0, 8, step, 0)

    def gather_levels(p, from_strip, from_half, strip, half):
        for near in range(4):
            level = (4 * p + near + 1) % Z
            for tile in range(2):
                rows = y[tile, pl.ds(piece(p, from_strip, from_half) + near, 18, stride=4), :]
                x[tile, pl.ds((strip * 2 + half) * CELL + level, 18, stride=8), :] = rows

    def put(strip, half):
        def put_row(inner, carry):
            for col in range(6):
                at = pl.multiple_of((strip * 2 + half) * CELL + (inner * 6 + col) * 8, 8)
                lane = (half * 6 + col) * C
                out[strip * 3 + inner, :, lane : lane + C] = take_rows(x, at, 8).astype(jnp.bfloat16)
            return carry

        lax.fori_loop(0, 3, put_row, 0)

    def take_home(i, slot, strip, half):
        for p in range(2):
            widen(y, p, *slot, returned[p, i])
            gather_levels(p, *slot, strip, half)

    for strip in range(3):
        for p in range(2):
            gather_levels(p, strip, 0, strip + 1, 1)
        put(strip + 1, 1)
    for copy in ahead:
        copy.wait_send()
    for block in range(2):
        for i in range(4):
            own_copy(block, i).wait_send()
        for i in range(3):
            passed_copy(block, i).wait_send()
        sibling_copy(block).wait_send()
    for copy in home[:6]:
        copy.wait()
    take_home(2, (2, 1), 3, 0)
    take_home(3, (3, 0), 0, 1)
    take_home(4, (3, 1), 0, 0)
    for where in ((3, 0), (0, 1), (0, 0)):
        put(*where)
    for copy in home[6:]:
        copy.wait()
    for strip in range(2):
        take_home(strip, (strip, 1), strip + 1, 0)
        put(strip + 1, 0)


def body(
    tokens,
    surface_ids,
    surface_embed,
    type_index,
    bias_plain,
    bias_shift,
    w_qkv,
    w_proj,
    w_up,
    w_down,
):
    spread = jnp.asarray(spread_matrix(), jnp.bfloat16)
    tail = jnp.asarray(query_tail(), jnp.float32)
    masks = jnp.asarray(mask_rows(), jnp.float32)
    lanes = jnp.asarray(head_lanes(), jnp.float32)
    in_vmem = pl.BlockSpec(memory_space=pltpu.VMEM)
    in_smem = pl.BlockSpec(memory_space=pltpu.SMEM)
    anywhere = pl.BlockSpec(memory_space=pl.ANY)
    rows = pl.pallas_call(
        kernel,
        out_shape=jax.ShapeDtypeStruct((ROWS, Z, COLS * C), jnp.bfloat16),
        in_specs=[anywhere, in_smem, in_smem]
        + [in_vmem] * 3
        + [anywhere]
        + [in_vmem] * 4
        + [anywhere] * 4,
        out_specs=in_vmem,
        scratch_shapes=[
            pltpu.VMEM((ROWS, Z, COLS * C), jnp.bfloat16),
            pltpu.VMEM((8, C), jnp.float32),
            pltpu.VMEM((2, 1104, 128), jnp.float32),
            pltpu.VMEM((4, 128, 384), jnp.bfloat16),
            pltpu.VMEM((3, 64, 128), jnp.float32),
            pltpu.VMEM((2, 48, 384), jnp.bfloat16),
            pltpu.VMEM((2, 6, 256, 256), jnp.bfloat16),
            pltpu.VMEM((2, 3 * C * C), jnp.bfloat16),
            pltpu.VMEM((2, C, HEADS * 128), jnp.bfloat16),
            pltpu.VMEM((2, C, C), jnp.bfloat16),
            pltpu.VMEM((2, C, 256), jnp.bfloat16),
            pltpu.VMEM((2, C, C), jnp.bfloat16),
            pltpu.VMEM((2, C, 4 * C), jnp.bfloat16),
            pltpu.VMEM((2, 4 * C, C), jnp.bfloat16),
            pltpu.VMEM((2, C * C), jnp.bfloat16),
            pltpu.VMEM((2, 4 * C * C), jnp.bfloat16),
            pltpu.VMEM((2, 3 * C * C // 128, 128), jnp.float32),
            pltpu.VMEM((2, C * C // 128, 128), jnp.float32),
            pltpu.VMEM((2, 4 * C * C // 128, 128), jnp.float32),
            pltpu.VMEM((5, 4 * C, 128), jnp.float32),
            pltpu.VMEM((2, 2, 4, 2, 48, 384), jnp.bfloat16),
            pltpu.VMEM((TABLES, WW, 16, 256), jnp.bfloat16),
            pltpu.VMEM((2, TOKENS, 128), jnp.float32),
            pltpu.VMEM((2, TOKENS, 128), jnp.float32),
            pltpu.VMEM((2, 2, 2, STRIPS, 80, C), jnp.bfloat16),
            pltpu.VMEM((2, 5, 80, C), jnp.bfloat16),
            pltpu.VMEM((2, 5, 80, C), jnp.bfloat16),
            pltpu.SemaphoreType.DMA((6,)),
            pltpu.SemaphoreType.DMA((2, 8)),
            pltpu.SemaphoreType.DMA((2, 8)),
            pltpu.SemaphoreType.DMA((15,)),
            pltpu.SemaphoreType.DMA((15,)),
        ],
        compiler_params=pltpu.CompilerParams(
            collective_id=0, has_side_effects=True, vmem_limit_bytes=56 * 1024 * 1024
        ),
    )(
        tokens.transpose(1, 0, 2),
        surface_ids,
        type_index,
        surface_embed,
        bias_plain.reshape(SHARD_LINES, 128),
        bias_shift.reshape(SHARD_LINES, 128),
        spread,
        tail,
        masks,
        lanes,
        jnp.asarray(head_spread(), jnp.bfloat16),
        w_qkv,
        w_proj,
        w_up,
        w_down,
    )
    return rows.transpose(1, 0, 2)


def solution(mesh):
    return jax.shard_map(
        body,
        mesh=mesh,
        in_specs=(
            P(None, "lat", "lon"),
            P("lat", "lon"),
            P(),
            P("lat"),
            P("lon"),
            P("lon"),
            P(),
            P(),
            P(),
            P(),
        ),
        out_specs=P(None, "lat", "lon"),
        check_vma=False,
    )
```

```python
import jax
import jax.numpy as jnp
import numpy as np
from jax import lax
from jax.experimental import pallas as pl
from jax.experimental.pallas import tpu as pltpu
from jax.sharding import PartitionSpec as P

HEADS = 6
HEAD_DIM = 32
C = 192
Z = 8
WZ = 2
WH = 6
WW = 12
ROWS = 12
COLS = 12
RELPOS = 3312
TYPES = 16
SPAN = 2 * WW - 1
STRIPS = 4
CELL = 144
TOKENS = 1152
HALF = 72
TABLES = 48
SHARD_LINES = 621
STRIDE = 69
CHUNKS = 18
KAPPA = WH * SPAN
LON = 16
BIG = 1e30
SCALE = HEAD_DIM**-0.5
PAIR = 2


def slot_positions():
    pos = np.arange(HALF)
    bh, ch, b3, c6 = pos // 36, pos // 18 % 2, pos // 6 % 3, pos % 6
    return bh * 3 + b3, ch * 6 + c6


def spread_matrix():
    b, c = slot_positions()
    out = np.zeros((2, 256, WW, 128), np.float32)
    for lane_type in range(2):
        for query_col in range(WW):
            row = b * SPAN + query_col - c + WW - 1 + lane_type * (KAPPA - 128)
            out[lane_type, row, query_col, np.arange(HALF)] = 1.0
    return out.reshape(2, 256, 6, 256).transpose(0, 2, 1, 3)


def query_tail():
    b, c = slot_positions()
    out = np.zeros((CELL, 256), np.float32)
    for a in range(2):
        rows = a * HALF + np.arange(HALF)
        out[rows, 32 + 16 * c + 8 * a + b] = 1.0
        out[rows, 224] = 1.0
        out[rows, 225 + a] = 1.0
        out[rows, 227 + b // 3] = 1.0
    return out


def mask_rows():
    b, _ = slot_positions()
    out = np.zeros((3, 32, 256), np.float32)
    for a in range(2):
        lanes = a * 128 + np.arange(HALF)
        out[0, 0, a * 128 + HALF : a * 128 + 128] = -BIG
        out[1, 1 + (1 - a), lanes] = -BIG
        out[2, 3 + (1 - b // 3), lanes] = -BIG
    return out


def head_lanes():
    out = np.zeros((HEADS + 1, 1, 256), np.float32)
    for head in range(HEADS):
        out[head, 0, head * HEAD_DIM : (head + 1) * HEAD_DIM] = 1.0
        out[head, 0, C + head] = 1.0
        out[HEADS, 0, C + head] = 1.0
    return out


def head_spread():
    out = np.zeros((256, C), np.float32)
    for head in range(HEADS):
        for row in (64 + head, 192 + head):
            out[row, head * HEAD_DIM : (head + 1) * HEAD_DIM] = 1.0
    return out


def normalised(x):
    center = jnp.sum(x, axis=-1, keepdims=True) * (1.0 / C)
    moved = x - center
    spread = jnp.sum(moved * moved, axis=-1, keepdims=True) * (1.0 / C)
    return moved * lax.rsqrt(spread + 1e-05)


def rounded(x):
    return x.astype(jnp.bfloat16).astype(jnp.float32)


def gelu(v):
    v = v.astype(jnp.bfloat16)
    first, third = jnp.bfloat16(0.7978845608028654), jnp.bfloat16(0.7978845608028654 * 0.044715)
    grown = jnp.tanh(v * (first + third * (v * v)))
    half = jnp.bfloat16(0.5) * v
    return half + half * grown


def dot(a, b):
    return jnp.dot(a, b, preferred_element_type=jnp.float32)


def dot_nt(a, b):
    return lax.dot_general(a, b, (((1,), (1,)), ((), ())), preferred_element_type=jnp.float32)


def row_of(level, lat_window):
    return (level // 4) * (TOKENS // 2) + lat_window * (HALF * 4) + lax.rem(level, 4)


def take_strided(ref, start):
    near = ref[0, pl.ds(start, HALF, stride=4), :]
    far = ref[1, pl.ds(start, HALF, stride=4), :]
    return jnp.concatenate([near, far[:, : C - 128]], axis=1)


def put_strided(ref, start, value):
    blank = jnp.zeros((HALF, 256 - C), jnp.float32)
    ref[0, pl.ds(start, HALF, stride=4), :] = value[:, :128]
    ref[1, pl.ds(start, HALF, stride=4), :] = jnp.concatenate([value[:, 128:], blank], axis=1)


def take_rows(ref, start, count):
    return jnp.concatenate(
        [ref[0, pl.ds(start, count), :], ref[1, pl.ds(start, count), : C - 128]], axis=1
    )


def put_rows(ref, start, value):
    rows = pl.ds(start, value.shape[0])
    ref[0, rows, :] = value[:, :128]
    ref[1, rows, : C - 128] = value[:, 128:]


def pick_types(block, lines, types, choose, ordered, picked):
    lane = lax.broadcasted_iota(jnp.int32, (1, 384), 1)
    second = lane >= KAPPA
    kappa = jnp.where(second, lane - KAPPA, lane)
    for phase in range(4):
        group = jnp.where(lane < 2 * KAPPA, (kappa + 2 * phase) // 8, -1)
        left = jnp.concatenate(
            [
                lines[block, pl.ds(17 * phase + chunk, 16, stride=STRIDE), :]
                for chunk in range(CHUNKS)
            ],
            axis=0,
        ).astype(jnp.bfloat16)
        wide = dot(left, choose[phase])
        total = jnp.zeros((16, 384), jnp.float32)
        for chunk in range(CHUNKS):
            total = jnp.where(group == chunk, wide[16 * chunk : 16 * chunk + 16], total)
        for tile in range(3):
            ordered[tile, pl.ds(phase, 16, stride=4), :] = total[:, 128 * tile : 128 * tile + 128]
    row = lax.broadcasted_iota(jnp.int32, (8, 384), 0)
    groups = []
    for group in range(6):
        whole = jnp.concatenate([ordered[tile, 6 * group : 6 * group + 8, :] for tile in range(3)], axis=1)
        groups.append(jnp.where(row < 6, whole, 0.0))
    picked[block] = jnp.concatenate(groups, axis=0).astype(jnp.bfloat16)


def choose_lanes(types, choose):
    lane = lax.broadcasted_iota(jnp.int32, (1, 384), 1)
    second = lane >= KAPPA
    kappa = jnp.where(second, lane - KAPPA, lane)
    wanted = jnp.where(second, types[1], types[0])
    row = lax.broadcasted_iota(jnp.int32, (128, 384), 0)
    for phase in range(4):
        target = lax.rem(kappa + 2 * phase, 8) * TYPES + wanted
        target = jnp.where(lane < 2 * KAPPA, target, -1)
        choose[phase] = (row == target).astype(jnp.float32).astype(jnp.bfloat16)


def to_lines(flat, lines):
    count = flat.shape[1] // 128

    def step(at, carry):
        start = pl.multiple_of(at * 2048, 2048)
        chunk = flat[:, pl.ds(start, 2048)].astype(jnp.float32)
        for j in range(16):
            for block in range(2):
                lines[block, pl.ds(at * 16 + j, 1), :] = chunk[
                    block : block + 1, 128 * j : 128 * j + 128
                ]
        return carry

    lax.fori_loop(0, count // 16, step, 0)


def to_matrix(lines, wide, block, rows, columns):
    period = 2 * columns // 128
    parts = [lines[block, pl.ds(j, rows // 2, stride=period), :] for j in range(period)]
    middle = period // 2
    full = columns // 128
    for tile in range(full):
        wide[tile, pl.ds(0, rows // 2, stride=2), :] = parts[tile]
        wide[tile, pl.ds(1, rows // 2, stride=2), :] = jnp.concatenate(
            [parts[middle + tile][:, 64:], parts[middle + tile + 1][:, :64]], axis=1
        )
    wide[full, pl.ds(0, rows // 2, stride=2), :] = parts[middle]
    last = parts[period - 1]
    wide[full, pl.ds(1, rows // 2, stride=2), :] = jnp.concatenate([last[:, 64:], last[:, :64]], axis=1)
    pieces = [wide[tile, 0:rows, :] for tile in range(full)] + [wide[full, 0:rows, 0:64]]
    return jnp.concatenate(pieces, axis=1).astype(jnp.bfloat16)


def prepare_weights(lines, wide, w_q, w_kt, w_v):
    lane = lax.broadcasted_iota(jnp.int32, (1, HEADS * 128), 1)
    inner = lax.rem(lane, 128)
    target = jnp.where(inner < HEAD_DIM, (lane // 128) * HEAD_DIM + inner, -1)
    row = lax.broadcasted_iota(jnp.int32, (C, HEADS * 128), 0)
    place = (row == target).astype(jnp.float32).astype(jnp.bfloat16)
    one = lax.broadcasted_iota(jnp.int32, (C, C), 0) == lax.broadcasted_iota(jnp.int32, (C, C), 1)
    one = one.astype(jnp.float32).astype(jnp.bfloat16)
    for block in range(2):
        qkv = to_matrix(lines, wide, block, C, 3 * C)
        w_q[block] = dot(qkv[:, 0:C], place).astype(jnp.bfloat16)
        w_kt[block] = dot_nt(one, qkv[:, C : 2 * C]).astype(jnp.bfloat16)
        blank = jnp.zeros((C, 256 - C), jnp.bfloat16)
        w_v[block] = jnp.concatenate([qkv[:, 2 * C : 3 * C], blank], axis=1)


def spread_tables(block, gathered, spread, tables):
    for lane_type in range(2):
        lanes = slice(128 * lane_type, 128 * lane_type + 256)
        left = jnp.concatenate(
            [
                gathered[block, c, x_of, z_of, :, lanes]
                for z_of in range(2)
                for x_of in range(4)
                for c in range(2)
            ],
            axis=0,
        )

        def step(pair, carry):
            wide = dot(left, spread[lane_type, pair])
            wide = wide.reshape(24, 2, 2, 8, 256)
            for inner in range(2):
                for a in range(2):
                    part = wide[:, :, a, :, 128 * inner : 128 * inner + 128]
                    part = part.reshape(24, 16, 128).astype(jnp.bfloat16)
                    tables[
                        24 * lane_type : 24 * lane_type + 24,
                        2 * pair + inner,
                        :,
                        128 * a : 128 * a + 128,
                    ] = part
            return carry

        lax.fori_loop(0, 6, step, 0, unroll=6)


def run_windows(block, lat_window, pair, x, y, tables, consts, weights, band):
    tail, masks, lanes, across_heads = consts
    w_q, w_kt, w_v, w_proj, w_up, w_down = weights
    last_band = (band == lax.axis_size("lat") - 1).astype(jnp.float32)
    shifted = block.astype(jnp.float32)
    starts, ends, level_windows = [], [], []
    for i in range(PAIR):
        level_window = pair * PAIR + i
        level_windows.append(level_window)
        for a in range(2):
            rolled = 2 * level_window + a
            level = lax.rem(rolled + block, Z)
            starts.append(row_of(level, lat_window))
            ends.append(row_of(rolled, lat_window))
    parts = [take_strided(x, s) for s in starts]
    stream = jnp.concatenate(parts, axis=0)
    normed = normalised(stream)
    normed_b = normed.astype(jnp.bfloat16)
    queries = dot(normed_b, w_q[block]) * SCALE
    blank = jnp.zeros((128 - HALF, C), jnp.float32)
    mixed_all = []
    for i in range(PAIR):
        first = normed[2 * i * HALF : (2 * i + 1) * HALF]
        second = normed[(2 * i + 1) * HALF : (2 * i + 2) * HALF]
        padded = jnp.concatenate([first, blank, second, blank], axis=0).astype(jnp.bfloat16)
        keys = dot_nt(w_kt[block], padded).astype(jnp.bfloat16)
        values = (dot(padded, w_v[block]) + lanes[HEADS]).astype(jnp.bfloat16)
        on_level = (level_windows[i] == 3).astype(jnp.float32) * shifted
        on_lat = (lat_window == 1).astype(jnp.float32) * last_band * shifted
        mask = masks[0] + masks[1] * on_level + masks[2] * on_lat
        mask = mask.astype(jnp.bfloat16)
        weight_parts, value_parts = [], []
        for head in range(HEADS):
            near = queries[i * CELL : (i + 1) * CELL, 128 * head : 128 * head + 128]
            near = (near + tail[:, 0:128]).astype(jnp.bfloat16)
            far = tail[:, 128:256].astype(jnp.bfloat16)
            left = jnp.concatenate([near, far], axis=1)
            table = tables[lat_window * 24 + level_windows[i] * HEADS + head].reshape(192, 256)
            right = jnp.concatenate([keys[32 * head : 32 * head + 32], table, mask], axis=0)
            scores = dot(left, right)
            top = jnp.max(scores, axis=-1, keepdims=True)
            weight_parts.append(jnp.exp((scores - top).astype(jnp.bfloat16)))
            value_parts.append(values * lanes[head].astype(jnp.bfloat16))
        mixed_all.append(
            dot(jnp.concatenate(weight_parts, axis=1), jnp.concatenate(value_parts, axis=0))
        )
    mixed = jnp.concatenate(mixed_all, axis=0)
    totals = mixed[:, 128:256]
    lane = lax.broadcasted_iota(jnp.int32, totals.shape, 1)
    counted = (lane >= C - 128) & (lane < C - 128 + HEADS)
    inverse = jnp.where(counted, 1.0 / totals, 0.0)
    coarse = inverse.astype(jnp.bfloat16)
    fine = (inverse - coarse.astype(jnp.float32)).astype(jnp.bfloat16)
    scale = dot(jnp.concatenate([coarse, fine], axis=1), across_heads[...])
    mixed = (mixed[:, :C] * scale).astype(jnp.bfloat16)
    middle = rounded(stream + dot(mixed, w_proj[block]))
    lifted = gelu(dot(normalised(middle).astype(jnp.bfloat16), w_up[block]))
    result = middle + dot(lifted, w_down[block])
    for j, s in enumerate(ends):
        put_strided(y, s, result[j * HALF : (j + 1) * HALF])


def kernel(
    tokens_hbm,
    ids,
    types,
    embed_in,
    bias_plain,
    bias_shift,
    spread_hbm,
    tail,
    masks,
    lanes,
    across_heads,
    qkv_hbm,
    proj_hbm,
    up_hbm,
    down_hbm,
    out,
    tokens,
    embed,
    lines,
    choose,
    ordered,
    picked,
    spread,
    qkv,
    w_q,
    w_kt,
    w_v,
    w_proj,
    w_up,
    w_down,
    flat_proj,
    flat_down,
    qkv_lines,
    proj_lines,
    down_lines,
    wide,
    gathered,
    tables,
    x,
    y,
    moved,
    received,
    returned,
    local_sems,
    gather_send,
    gather_recv,
    halo_send,
    halo_recv,
):
    lat, lon = lax.axis_index("lat"), lax.axis_index("lon")
    lats, lons = lax.axis_size("lat"), lax.axis_size("lon")
    consts = (tail, masks, lanes, across_heads)
    weights = (w_q, w_kt, w_v, w_proj, w_up, w_down)
    north, south = lax.rem(lat + lats - 1, lats), lax.rem(lat + 1, lats)
    west, east = lax.rem(lon + lons - 1, lons), lax.rem(lon + 1, lons)

    sources = (tokens_hbm, qkv_hbm, spread_hbm, proj_hbm, up_hbm, down_hbm)
    targets = (tokens, qkv, spread, flat_proj, w_up, flat_down)
    loads = [
        pltpu.make_async_copy(source, target, local_sems.at[i])
        for i, (source, target) in enumerate(zip(sources, targets))
    ]
    for load in loads:
        load.start()

    def place(i, j):
        return {"lat": i, "lon": j}

    crosses, sides = 2, 2
    across = lons // (crosses * sides)
    core, x_at, z_at = lax.rem(lon, sides), lax.rem(lon // sides, across), lon // (sides * across)

    def lon_of(z, x, c):
        return (z * across + x) * sides + c

    opposite = lon_of(1 - z_at, x_at, core)
    sibling = lon_of(z_at, x_at, 1 - core)
    peers = [lon_of(z_at, lax.rem(x_at + step, across), core) for step in range(1, 4)]
    origins = [lax.rem(x_at + across - step, across) for step in range(1, 4)]
    partners = [(lat, j) for j in (opposite, sibling, *peers, west, east)]
    partners += [(north, lon), (south, lon), (north, west), (south, east)]

    barrier = pltpu.get_barrier_semaphore()
    for i, j in partners:
        pl.semaphore_signal(
            barrier, inc=1, device_id=place(i, j), device_id_type=pl.DeviceIdType.MESH
        )

    def share(block, index, source, slot, target):
        return pltpu.make_async_remote_copy(
            src_ref=source,
            dst_ref=slot,
            send_sem=gather_send.at[block, index],
            recv_sem=gather_recv.at[block, index],
            device_id=place(lat, target),
            device_id_type=pl.DeviceIdType.MESH,
        )

    def slot(block, x_of, z_of):
        return gathered.at[block, core, x_of, z_of]

    def own_copy(block, i):
        target = opposite if i == 0 else peers[i - 1]
        return share(block, i, picked.at[block], slot(block, x_at, z_at), target)

    def passed_copy(block, i):
        held = slot(block, x_at, 1 - z_at)
        return share(block, 4 + i, held, held, peers[i])

    def sibling_copy(block, part):
        held = gathered.at[block, core, :, z_at if part == 0 else 1 - z_at]
        return share(block, 7 + part, held, held, sibling)

    def wait_opposite(block):
        share(block, 0, picked.at[block], slot(block, x_at, 1 - z_at), opposite).wait_recv()

    def near_part(block):
        for i, origin in enumerate(origins):
            share(block, 1 + i, picked.at[block], slot(block, origin, z_at), lon).wait_recv()
        sibling_copy(block, 0).start()

    def far_part(block):
        for i, origin in enumerate(origins):
            share(block, 4 + i, picked.at[block], slot(block, origin, 1 - z_at), lon).wait_recv()
        sibling_copy(block, 1).start()

    def wait_sibling(block):
        for part in range(2):
            other = gathered.at[block, 1 - core, :, z_at if part == 0 else 1 - z_at]
            share(block, 7 + part, other, other, sibling).wait_recv()

    lines[0, 0:SHARD_LINES] = bias_plain[...].astype(jnp.float32)
    lines[1, 0:SHARD_LINES] = bias_shift[...].astype(jnp.float32)
    choose_lanes(types, choose)
    pl.semaphore_wait(barrier, len(partners))

    def pick_and_send(block):
        pick_types(block, lines, types, choose, ordered, picked)
        for i in range(4):
            own_copy(block, i).start()
        gathered[block, core, x_at, z_at] = picked[block]

    pick_and_send(0)

    embed[0:3, :] = embed_in[...].astype(jnp.float32)
    loads[0].wait()

    def embed_row(row, carry):
        strip, inner = row // 3, row % 3
        for col in range(0, COLS, 2):
            cells = []
            for c in (col, col + 1):
                cell = tokens[row, :, C * c : C * c + C].astype(jnp.float32)
                cells.append(rounded(cell + embed[pl.ds(ids[row, c], 1), :]))
            for part in range(2):
                start = part * (TOKENS // 2) + (strip * 2 + col // 6) * HALF
                start = pl.multiple_of(start + (inner * 6 + col % 6) * 4, 8)
                rows = [cell[4 * part : 4 * part + 4] for cell in cells]
                put_rows(x, start, jnp.concatenate(rows, axis=0))
        return carry

    lax.fori_loop(0, ROWS, embed_row, 0)

    def pass_on(block):
        wait_opposite(block)
        for i in range(3):
            passed_copy(block, i).start()

    pass_on(0)
    loads[1].wait()
    to_lines(qkv, qkv_lines)
    prepare_weights(qkv_lines, wide, w_q, w_kt, w_v)
    loads[3].wait()
    to_lines(flat_proj, proj_lines)
    for block in range(2):
        w_proj[block] = to_matrix(proj_lines, wide, block, C, C)
    near_part(0)
    pick_and_send(1)
    far_part(0)
    loads[5].wait()
    to_lines(flat_down, down_lines)
    for block in range(2):
        w_down[block] = to_matrix(down_lines, wide, block, 4 * C, C)
    loads[2].wait()
    loads[4].wait()

    def halo(index, source, target, i, j):
        return pltpu.make_async_remote_copy(
            src_ref=source,
            dst_ref=target,
            send_sem=halo_send.at[index],
            recv_sem=halo_recv.at[index],
            device_id=place(i, j),
            device_id_type=pl.DeviceIdType.MESH,
        )

    sent, back = moved.at[0], moved.at[1]
    ahead = [
        halo(0, sent.at[:, 0, 0], received.at[:, 4], north, west),
        halo(1, sent.at[:, 1, 0], received.at[:, 3], north, lon),
        halo(2, sent.at[:, 0, 1], received.at[:, 0], lat, west),
    ]
    ahead += [halo(3 + p, sent.at[p, 0, 3], received.at[p, 2], lat, west) for p in range(2)]
    ahead += [halo(5 + p, sent.at[p, 0, 2], received.at[p, 1], lat, west) for p in range(2)]
    home = []
    for p in range(2):
        home += [
            halo(7 + 3 * p, back.at[p, 1, 3], returned.at[p, 4], south, east),
            halo(8 + 3 * p, back.at[p, 0, 3], returned.at[p, 3], south, lon),
            halo(9 + 3 * p, back.at[p, 1, 2], returned.at[p, 2], lat, east),
        ]
    home += [halo(13 + p, back.at[p, 1, 0:2], returned.at[p, 0:2], lat, east) for p in range(2)]

    def piece(p, strip, half):
        return p * (TOKENS // 2) + (strip * 2 + half) * HALF

    def narrow(block, p, lat_window):
        blank = jnp.zeros((80 - HALF, C), jnp.float32)
        for bh in range(2):
            for half in range(2):
                strip = 2 * lat_window + bh
                rows = take_rows(y, pl.multiple_of(piece(p, strip, half), 8), HALF)
                rows = jnp.concatenate([rows, blank], axis=0)
                moved[block, p, half, strip] = rows.astype(jnp.bfloat16)

    def widen(target, p, strip, half, source):
        put_rows(target, piece(p, strip, half), source.astype(jnp.float32)[:HALF])

    def step(at, carry):
        stage, pair = at // 2, lax.rem(at, 2)
        block = stage // 2
        lat_window = jnp.where(block == 0, stage, 3 - stage)

        @pl.when(lax.rem(at, 4) == 0)
        def _():
            wait_sibling(block)
            spread_tables(block, gathered, spread, tables)

        @pl.when(at == 4)
        def _():
            for p in range(2):
                widen(x, p, 2, 0, sent[p, 1, 3])
            for i in (0, 1, 3, 4):
                ahead[i].wait_recv()
            for p in range(2):
                widen(x, p, 2, 1, received[p, 2])
                widen(x, p, 3, 0, received[p, 3])
                widen(x, p, 3, 1, received[p, 4])

        @pl.when(at == 6)
        def _():
            for p in range(2):
                widen(x, p, 0, 0, sent[p, 1, 1])
                widen(x, p, 1, 0, sent[p, 1, 2])
            for i in (2, 5, 6):
                ahead[i].wait_recv()
            for p in range(2):
                widen(x, p, 0, 1, received[p, 0])
                widen(x, p, 1, 1, received[p, 1])

        run_windows(block, lat_window, pair, x, y, tables, consts, weights, lat)

        narrow(block, pair, lat_window)

        def after(when, copies):
            @pl.when(at == when)
            def _():
                for copy in copies:
                    copy.start()

        after(1, ahead[0:3])
        after(2, [ahead[3], ahead[5]])
        after(3, [ahead[4], ahead[6]])
        after(4, home[0:3])
        after(5, home[3:6])
        after(6, home[6:7])
        after(7, home[7:8])

        @pl.when(at == 0)
        def _():
            pass_on(1)

        @pl.when(at == 1)
        def _():
            near_part(1)
            far_part(1)

        return carry

    lax.fori_loop(0, 8, step, 0)

    def gather_levels(p, from_strip, from_half, strip, half):
        for near in range(4):
            level = (4 * p + near + 1) % Z
            for tile in range(2):
                rows = y[tile, pl.ds(piece(p, from_strip, from_half) + near, 18, stride=4), :]
                x[tile, pl.ds((strip * 2 + half) * CELL + level, 18, stride=8), :] = rows

    def put(strip, half):
        def put_row(inner, carry):
            for col in range(6):
                at = pl.multiple_of((strip * 2 + half) * CELL + (inner * 6 + col) * 8, 8)
                lane = (half * 6 + col) * C
                out[strip * 3 + inner, :, lane : lane + C] = take_rows(x, at, 8).astype(jnp.bfloat16)
            return carry

        lax.fori_loop(0, 3, put_row, 0)

    def take_home(i, slot, strip, half):
        for p in range(2):
            widen(y, p, *slot, returned[p, i])
            gather_levels(p, *slot, strip, half)

    for strip in range(3):
        for p in range(2):
            gather_levels(p, strip, 0, strip + 1, 1)
        put(strip + 1, 1)
    for copy in ahead:
        copy.wait_send()
    for block in range(2):
        for i in range(4):
            own_copy(block, i).wait_send()
        for i in range(3):
            passed_copy(block, i).wait_send()
        for part in range(2):
            sibling_copy(block, part).wait_send()
    for copy in home[:6]:
        copy.wait()
    take_home(2, (2, 1), 3, 0)
    take_home(3, (3, 0), 0, 1)
    take_home(4, (3, 1), 0, 0)
    for where in ((3, 0), (0, 1), (0, 0)):
        put(*where)
    for copy in home[6:]:
        copy.wait()
    for strip in range(2):
        take_home(strip, (strip, 1), strip + 1, 0)
        put(strip + 1, 0)


def body(
    tokens,
    surface_ids,
    surface_embed,
    type_index,
    bias_plain,
    bias_shift,
    w_qkv,
    w_proj,
    w_up,
    w_down,
):
    spread = jnp.asarray(spread_matrix(), jnp.bfloat16)
    tail = jnp.asarray(query_tail(), jnp.float32)
    masks = jnp.asarray(mask_rows(), jnp.float32)
    lanes = jnp.asarray(head_lanes(), jnp.float32)
    in_vmem = pl.BlockSpec(memory_space=pltpu.VMEM)
    in_smem = pl.BlockSpec(memory_space=pltpu.SMEM)
    anywhere = pl.BlockSpec(memory_space=pl.ANY)
    rows = pl.pallas_call(
        kernel,
        out_shape=jax.ShapeDtypeStruct((ROWS, Z, COLS * C), jnp.bfloat16),
        in_specs=[anywhere, in_smem, in_smem]
        + [in_vmem] * 3
        + [anywhere]
        + [in_vmem] * 4
        + [anywhere] * 4,
        out_specs=in_vmem,
        scratch_shapes=[
            pltpu.VMEM((ROWS, Z, COLS * C), jnp.bfloat16),
            pltpu.VMEM((8, C), jnp.float32),
            pltpu.VMEM((2, 1104, 128), jnp.float32),
            pltpu.VMEM((4, 128, 384), jnp.bfloat16),
            pltpu.VMEM((3, 64, 128), jnp.float32),
            pltpu.VMEM((2, 48, 384), jnp.bfloat16),
            pltpu.VMEM((2, 6, 256, 256), jnp.bfloat16),
            pltpu.VMEM((2, 3 * C * C), jnp.bfloat16),
            pltpu.VMEM((2, C, HEADS * 128), jnp.bfloat16),
            pltpu.VMEM((2, C, C), jnp.bfloat16),
            pltpu.VMEM((2, C, 256), jnp.bfloat16),
            pltpu.VMEM((2, C, C), jnp.bfloat16),
            pltpu.VMEM((2, C, 4 * C), jnp.bfloat16),
            pltpu.VMEM((2, 4 * C, C), jnp.bfloat16),
            pltpu.VMEM((2, C * C), jnp.bfloat16),
            pltpu.VMEM((2, 4 * C * C), jnp.bfloat16),
            pltpu.VMEM((2, 3 * C * C // 128, 128), jnp.float32),
            pltpu.VMEM((2, C * C // 128, 128), jnp.float32),
            pltpu.VMEM((2, 4 * C * C // 128, 128), jnp.float32),
            pltpu.VMEM((5, 4 * C, 128), jnp.float32),
            pltpu.VMEM((2, 2, 4, 2, 48, 384), jnp.bfloat16),
            pltpu.VMEM((TABLES, WW, 16, 256), jnp.bfloat16),
            pltpu.VMEM((2, TOKENS, 128), jnp.float32),
            pltpu.VMEM((2, TOKENS, 128), jnp.float32),
            pltpu.VMEM((2, 2, 2, STRIPS, 80, C), jnp.bfloat16),
            pltpu.VMEM((2, 5, 80, C), jnp.bfloat16),
            pltpu.VMEM((2, 5, 80, C), jnp.bfloat16),
            pltpu.SemaphoreType.DMA((6,)),
            pltpu.SemaphoreType.DMA((2, 9)),
            pltpu.SemaphoreType.DMA((2, 9)),
            pltpu.SemaphoreType.DMA((15,)),
            pltpu.SemaphoreType.DMA((15,)),
        ],
        compiler_params=pltpu.CompilerParams(
            collective_id=0, has_side_effects=True, vmem_limit_bytes=56 * 1024 * 1024
        ),
    )(
        tokens.transpose(1, 0, 2),
        surface_ids,
        type_index,
        surface_embed,
        bias_plain.reshape(SHARD_LINES, 128),
        bias_shift.reshape(SHARD_LINES, 128),
        spread,
        tail,
        masks,
        lanes,
        jnp.asarray(head_spread(), jnp.bfloat16),
        w_qkv,
        w_proj,
        w_up,
        w_down,
    )
    return rows.transpose(1, 0, 2)


def solution(mesh):
    return jax.shard_map(
        body,
        mesh=mesh,
        in_specs=(
            P(None, "lat", "lon"),
            P("lat", "lon"),
            P(),
            P("lat"),
            P("lon"),
            P("lon"),
            P(),
            P(),
            P(),
            P(),
        ),
        out_specs=P(None, "lat", "lon"),
        check_vma=False,
    )
```

```python
import jax
import jax.numpy as jnp
import numpy as np
from jax import lax
from jax.experimental import pallas as pl
from jax.experimental.pallas import tpu as pltpu
from jax.sharding import PartitionSpec as P

HEADS = 6
HEAD_DIM = 32
C = 192
Z = 8
WZ = 2
WH = 6
WW = 12
ROWS = 12
COLS = 12
RELPOS = 3312
TYPES = 16
SPAN = 2 * WW - 1
STRIPS = 4
CELL = 144
TOKENS = 1152
HALF = 72
TABLES = 48
SHARD_LINES = 621
STRIDE = 69
CHUNKS = 18
KAPPA = WH * SPAN
LON = 16
BIG = 1e30
SCALE = HEAD_DIM**-0.5
PAIR = 4


def slot_positions():
    pos = np.arange(HALF)
    bh, ch, b3, c6 = pos // 36, pos // 18 % 2, pos // 6 % 3, pos % 6
    return bh * 3 + b3, ch * 6 + c6


def spread_matrix():
    b, c = slot_positions()
    out = np.zeros((2, 256, WW, 128), np.float32)
    for lane_type in range(2):
        for query_col in range(WW):
            row = b * SPAN + query_col - c + WW - 1 + lane_type * (KAPPA - 128)
            out[lane_type, row, query_col, np.arange(HALF)] = 1.0
    return out.reshape(2, 256, 6, 256).transpose(0, 2, 1, 3)


def query_tail():
    b, c = slot_positions()
    out = np.zeros((CELL, 256), np.float32)
    for a in range(2):
        rows = a * HALF + np.arange(HALF)
        out[rows, 32 + 16 * c + 8 * a + b] = 1.0
        out[rows, 224] = 1.0
        out[rows, 225 + a] = 1.0
        out[rows, 227 + b // 3] = 1.0
    return out


def mask_rows():
    b, _ = slot_positions()
    out = np.zeros((3, 32, 256), np.float32)
    for a in range(2):
        lanes = a * 128 + np.arange(HALF)
        out[0, 0, a * 128 + HALF : a * 128 + 128] = -BIG
        out[1, 1 + (1 - a), lanes] = -BIG
        out[2, 3 + (1 - b // 3), lanes] = -BIG
    return out


def head_lanes():
    out = np.zeros((HEADS + 1, 1, 256), np.float32)
    for head in range(HEADS):
        out[head, 0, head * HEAD_DIM : (head + 1) * HEAD_DIM] = 1.0
        out[head, 0, C + head] = 1.0
        out[HEADS, 0, C + head] = 1.0
    return out


def head_spread():
    out = np.zeros((256, C), np.float32)
    for head in range(HEADS):
        for row in (64 + head, 192 + head):
            out[row, head * HEAD_DIM : (head + 1) * HEAD_DIM] = 1.0
    return out


def normalised(x):
    center = jnp.sum(x, axis=-1, keepdims=True) * (1.0 / C)
    moved = x - center
    spread = jnp.sum(moved * moved, axis=-1, keepdims=True) * (1.0 / C)
    return moved * lax.rsqrt(spread + 1e-05)


def rounded(x):
    return x.astype(jnp.bfloat16).astype(jnp.float32)


def gelu(v):
    v = v.astype(jnp.bfloat16)
    first, third = jnp.bfloat16(0.7978845608028654), jnp.bfloat16(0.7978845608028654 * 0.044715)
    grown = jnp.tanh(v * (first + third * (v * v)))
    half = jnp.bfloat16(0.5) * v
    return half + half * grown


def dot(a, b):
    return jnp.dot(a, b, preferred_element_type=jnp.float32)


def dot_nt(a, b):
    return lax.dot_general(a, b, (((1,), (1,)), ((), ())), preferred_element_type=jnp.float32)


def row_of(level, lat_window):
    return (level // 4) * (TOKENS // 2) + lat_window * (HALF * 4) + lax.rem(level, 4)


def take_strided(ref, start):
    near = ref[0, pl.ds(start, HALF, stride=4), :]
    far = ref[1, pl.ds(start, HALF, stride=4), :]
    return jnp.concatenate([near, far[:, : C - 128]], axis=1)


def put_strided(ref, start, value):
    blank = jnp.zeros((HALF, 256 - C), jnp.float32)
    ref[0, pl.ds(start, HALF, stride=4), :] = value[:, :128]
    ref[1, pl.ds(start, HALF, stride=4), :] = jnp.concatenate([value[:, 128:], blank], axis=1)


def take_rows(ref, start, count):
    return jnp.concatenate(
        [ref[0, pl.ds(start, count), :], ref[1, pl.ds(start, count), : C - 128]], axis=1
    )


def put_rows(ref, start, value):
    rows = pl.ds(start, value.shape[0])
    ref[0, rows, :] = value[:, :128]
    ref[1, rows, : C - 128] = value[:, 128:]


def pick_types(block, lines, types, choose, ordered, picked):
    lane = lax.broadcasted_iota(jnp.int32, (1, 384), 1)
    second = lane >= KAPPA
    kappa = jnp.where(second, lane - KAPPA, lane)
    for phase in range(4):
        group = jnp.where(lane < 2 * KAPPA, (kappa + 2 * phase) // 8, -1)
        left = jnp.concatenate(
            [
                lines[block, pl.ds(17 * phase + chunk, 16, stride=STRIDE), :]
                for chunk in range(CHUNKS)
            ],
            axis=0,
        ).astype(jnp.bfloat16)
        wide = dot(left, choose[phase])
        total = jnp.zeros((16, 384), jnp.float32)
        for chunk in range(CHUNKS):
            total = jnp.where(group == chunk, wide[16 * chunk : 16 * chunk + 16], total)
        for tile in range(3):
            ordered[tile, pl.ds(phase, 16, stride=4), :] = total[:, 128 * tile : 128 * tile + 128]
    row = lax.broadcasted_iota(jnp.int32, (8, 384), 0)
    groups = []
    for group in range(6):
        whole = jnp.concatenate([ordered[tile, 6 * group : 6 * group + 8, :] for tile in range(3)], axis=1)
        groups.append(jnp.where(row < 6, whole, 0.0))
    picked[block] = jnp.concatenate(groups, axis=0).astype(jnp.bfloat16)


def choose_lanes(types, choose):
    lane = lax.broadcasted_iota(jnp.int32, (1, 384), 1)
    second = lane >= KAPPA
    kappa = jnp.where(second, lane - KAPPA, lane)
    wanted = jnp.where(second, types[1], types[0])
    row = lax.broadcasted_iota(jnp.int32, (128, 384), 0)
    for phase in range(4):
        target = lax.rem(kappa + 2 * phase, 8) * TYPES + wanted
        target = jnp.where(lane < 2 * KAPPA, target, -1)
        choose[phase] = (row == target).astype(jnp.float32).astype(jnp.bfloat16)


def to_lines(flat, lines):
    count = flat.shape[1] // 128

    def step(at, carry):
        start = pl.multiple_of(at * 2048, 2048)
        chunk = flat[:, pl.ds(start, 2048)].astype(jnp.float32)
        for j in range(16):
            for block in range(2):
                lines[block, pl.ds(at * 16 + j, 1), :] = chunk[
                    block : block + 1, 128 * j : 128 * j + 128
                ]
        return carry

    lax.fori_loop(0, count // 16, step, 0)


def to_matrix(lines, wide, block, rows, columns):
    period = 2 * columns // 128
    parts = [lines[block, pl.ds(j, rows // 2, stride=period), :] for j in range(period)]
    middle = period // 2
    full = columns // 128
    for tile in range(full):
        wide[tile, pl.ds(0, rows // 2, stride=2), :] = parts[tile]
        wide[tile, pl.ds(1, rows // 2, stride=2), :] = jnp.concatenate(
            [parts[middle + tile][:, 64:], parts[middle + tile + 1][:, :64]], axis=1
        )
    wide[full, pl.ds(0, rows // 2, stride=2), :] = parts[middle]
    last = parts[period - 1]
    wide[full, pl.ds(1, rows // 2, stride=2), :] = jnp.concatenate([last[:, 64:], last[:, :64]], axis=1)
    pieces = [wide[tile, 0:rows, :] for tile in range(full)] + [wide[full, 0:rows, 0:64]]
    return jnp.concatenate(pieces, axis=1).astype(jnp.bfloat16)


def prepare_weights(lines, wide, w_q, w_kt, w_v):
    lane = lax.broadcasted_iota(jnp.int32, (1, HEADS * 128), 1)
    inner = lax.rem(lane, 128)
    target = jnp.where(inner < HEAD_DIM, (lane // 128) * HEAD_DIM + inner, -1)
    row = lax.broadcasted_iota(jnp.int32, (C, HEADS * 128), 0)
    place = (row == target).astype(jnp.float32).astype(jnp.bfloat16)
    one = lax.broadcasted_iota(jnp.int32, (C, C), 0) == lax.broadcasted_iota(jnp.int32, (C, C), 1)
    one = one.astype(jnp.float32).astype(jnp.bfloat16)
    for block in range(2):
        qkv = to_matrix(lines, wide, block, C, 3 * C)
        w_q[block] = dot(qkv[:, 0:C], place).astype(jnp.bfloat16)
        w_kt[block] = dot_nt(one, qkv[:, C : 2 * C]).astype(jnp.bfloat16)
        blank = jnp.zeros((C, 256 - C), jnp.bfloat16)
        w_v[block] = jnp.concatenate([qkv[:, 2 * C : 3 * C], blank], axis=1)


def spread_tables(block, gathered, spread, tables):
    for lane_type in range(2):
        lanes = slice(128 * lane_type, 128 * lane_type + 256)
        left = jnp.concatenate(
            [
                gathered[block, c, x_of, z_of, :, lanes]
                for z_of in range(2)
                for x_of in range(4)
                for c in range(2)
            ],
            axis=0,
        )

        def step(pair, carry):
            wide = dot(left, spread[lane_type, pair])
            wide = wide.reshape(24, 2, 2, 8, 256)
            for inner in range(2):
                for a in range(2):
                    part = wide[:, :, a, :, 128 * inner : 128 * inner + 128]
                    part = part.reshape(24, 16, 128).astype(jnp.bfloat16)
                    tables[
                        24 * lane_type : 24 * lane_type + 24,
                        2 * pair + inner,
                        :,
                        128 * a : 128 * a + 128,
                    ] = part
            return carry

        lax.fori_loop(0, 6, step, 0, unroll=6)


def run_windows(block, lat_window, pair, x, y, tables, consts, weights, band):
    tail, masks, lanes, across_heads = consts
    w_q, w_kt, w_v, w_proj, w_up, w_down = weights
    last_band = (band == lax.axis_size("lat") - 1).astype(jnp.float32)
    shifted = block.astype(jnp.float32)
    starts, ends, level_windows = [], [], []
    for i in range(PAIR):
        level_window = pair * PAIR + i
        level_windows.append(level_window)
        for a in range(2):
            rolled = 2 * level_window + a
            level = lax.rem(rolled + block, Z)
            starts.append(row_of(level, lat_window))
            ends.append(row_of(rolled, lat_window))
    parts = [take_strided(x, s) for s in starts]
    stream = jnp.concatenate(parts, axis=0)
    normed = normalised(stream)
    normed_b = normed.astype(jnp.bfloat16)
    queries = dot(normed_b, w_q[block]) * SCALE
    blank = jnp.zeros((128 - HALF, C), jnp.float32)
    mixed_all = []
    for i in range(PAIR):
        first = normed[2 * i * HALF : (2 * i + 1) * HALF]
        second = normed[(2 * i + 1) * HALF : (2 * i + 2) * HALF]
        padded = jnp.concatenate([first, blank, second, blank], axis=0).astype(jnp.bfloat16)
        keys = dot_nt(w_kt[block], padded).astype(jnp.bfloat16)
        values = (dot(padded, w_v[block]) + lanes[HEADS]).astype(jnp.bfloat16)
        on_level = (level_windows[i] == 3).astype(jnp.float32) * shifted
        on_lat = (lat_window == 1).astype(jnp.float32) * last_band * shifted
        mask = masks[0] + masks[1] * on_level + masks[2] * on_lat
        mask = mask.astype(jnp.bfloat16)
        weight_parts, value_parts = [], []
        for head in range(HEADS):
            near = queries[i * CELL : (i + 1) * CELL, 128 * head : 128 * head + 128]
            near = (near + tail[:, 0:128]).astype(jnp.bfloat16)
            far = tail[:, 128:256].astype(jnp.bfloat16)
            left = jnp.concatenate([near, far], axis=1)
            table = tables[lat_window * 24 + level_windows[i] * HEADS + head].reshape(192, 256)
            right = jnp.concatenate([keys[32 * head : 32 * head + 32], table, mask], axis=0)
            scores = dot(left, right)
            top = jnp.max(scores, axis=-1, keepdims=True)
            weight_parts.append(jnp.exp((scores - top).astype(jnp.bfloat16)))
            value_parts.append(values * lanes[head].astype(jnp.bfloat16))
        mixed_all.append(
            dot(jnp.concatenate(weight_parts, axis=1), jnp.concatenate(value_parts, axis=0))
        )
    mixed = jnp.concatenate(mixed_all, axis=0)
    totals = mixed[:, 128:256]
    lane = lax.broadcasted_iota(jnp.int32, totals.shape, 1)
    counted = (lane >= C - 128) & (lane < C - 128 + HEADS)
    inverse = jnp.where(counted, 1.0 / totals, 0.0)
    coarse = inverse.astype(jnp.bfloat16)
    fine = (inverse - coarse.astype(jnp.float32)).astype(jnp.bfloat16)
    scale = dot(jnp.concatenate([coarse, fine], axis=1), across_heads[...])
    mixed = (mixed[:, :C] * scale).astype(jnp.bfloat16)
    middle = rounded(stream + dot(mixed, w_proj[block]))
    lifted = gelu(dot(normalised(middle).astype(jnp.bfloat16), w_up[block]))
    result = middle + dot(lifted, w_down[block])
    for j, s in enumerate(ends):
        put_strided(y, s, result[j * HALF : (j + 1) * HALF])


def kernel(
    tokens_hbm,
    ids,
    types,
    embed_in,
    bias_plain,
    bias_shift,
    spread_hbm,
    tail,
    masks,
    lanes,
    across_heads,
    qkv_hbm,
    proj_hbm,
    up_hbm,
    down_hbm,
    out,
    tokens,
    embed,
    lines,
    choose,
    ordered,
    picked,
    spread,
    qkv,
    w_q,
    w_kt,
    w_v,
    w_proj,
    w_up,
    w_down,
    flat_proj,
    flat_down,
    qkv_lines,
    proj_lines,
    down_lines,
    wide,
    gathered,
    tables,
    x,
    y,
    moved,
    received,
    returned,
    local_sems,
    gather_send,
    gather_recv,
    halo_send,
    halo_recv,
):
    lat, lon = lax.axis_index("lat"), lax.axis_index("lon")
    lats, lons = lax.axis_size("lat"), lax.axis_size("lon")
    consts = (tail, masks, lanes, across_heads)
    weights = (w_q, w_kt, w_v, w_proj, w_up, w_down)
    north, south = lax.rem(lat + lats - 1, lats), lax.rem(lat + 1, lats)
    west, east = lax.rem(lon + lons - 1, lons), lax.rem(lon + 1, lons)

    sources = (tokens_hbm, qkv_hbm, spread_hbm, proj_hbm, up_hbm, down_hbm)
    targets = (tokens, qkv, spread, flat_proj, w_up, flat_down)
    loads = [
        pltpu.make_async_copy(source, target, local_sems.at[i])
        for i, (source, target) in enumerate(zip(sources, targets))
    ]
    for load in loads:
        load.start()

    def place(i, j):
        return {"lat": i, "lon": j}

    crosses, sides = 2, 2
    across = lons // (crosses * sides)
    core, x_at, z_at = lax.rem(lon, sides), lax.rem(lon // sides, across), lon // (sides * across)

    def lon_of(z, x, c):
        return (z * across + x) * sides + c

    opposite = lon_of(1 - z_at, x_at, core)
    sibling = lon_of(z_at, x_at, 1 - core)
    peers = [lon_of(z_at, lax.rem(x_at + step, across), core) for step in range(1, 4)]
    origins = [lax.rem(x_at + across - step, across) for step in range(1, 4)]
    partners = [(lat, j) for j in (opposite, sibling, *peers, west, east)]
    partners += [(north, lon), (south, lon), (north, west), (south, east)]

    barrier = pltpu.get_barrier_semaphore()
    for i, j in partners:
        pl.semaphore_signal(
            barrier, inc=1, device_id=place(i, j), device_id_type=pl.DeviceIdType.MESH
        )

    def share(block, index, source, slot, target):
        return pltpu.make_async_remote_copy(
            src_ref=source,
            dst_ref=slot,
            send_sem=gather_send.at[block, index],
            recv_sem=gather_recv.at[block, index],
            device_id=place(lat, target),
            device_id_type=pl.DeviceIdType.MESH,
        )

    def slot(block, x_of, z_of):
        return gathered.at[block, core, x_of, z_of]

    def own_copy(block, i):
        target = opposite if i == 0 else peers[i - 1]
        return share(block, i, picked.at[block], slot(block, x_at, z_at), target)

    def passed_copy(block, i):
        held = slot(block, x_at, 1 - z_at)
        return share(block, 4 + i, held, held, peers[i])

    def sibling_copy(block, part):
        held = gathered.at[block, core, :, z_at if part == 0 else 1 - z_at]
        return share(block, 7 + part, held, held, sibling)

    def wait_opposite(block):
        share(block, 0, picked.at[block], slot(block, x_at, 1 - z_at), opposite).wait_recv()

    def near_part(block):
        for i, origin in enumerate(origins):
            share(block, 1 + i, picked.at[block], slot(block, origin, z_at), lon).wait_recv()
        sibling_copy(block, 0).start()

    def far_part(block):
        for i, origin in enumerate(origins):
            share(block, 4 + i, picked.at[block], slot(block, origin, 1 - z_at), lon).wait_recv()
        sibling_copy(block, 1).start()

    def wait_sibling(block):
        for part in range(2):
            other = gathered.at[block, 1 - core, :, z_at if part == 0 else 1 - z_at]
            share(block, 7 + part, other, other, sibling).wait_recv()

    lines[0, 0:SHARD_LINES] = bias_plain[...].astype(jnp.float32)
    lines[1, 0:SHARD_LINES] = bias_shift[...].astype(jnp.float32)
    choose_lanes(types, choose)
    pl.semaphore_wait(barrier, len(partners))

    def pick_and_send(block):
        pick_types(block, lines, types, choose, ordered, picked)
        for i in range(4):
            own_copy(block, i).start()
        gathered[block, core, x_at, z_at] = picked[block]

    pick_and_send(0)

    embed[0:3, :] = embed_in[...].astype(jnp.float32)
    loads[0].wait()

    def embed_row(row, carry):
        strip, inner = row // 3, row % 3
        for col in range(0, COLS, 2):
            cells = []
            for c in (col, col + 1):
                cell = tokens[row, :, C * c : C * c + C].astype(jnp.float32)
                cells.append(rounded(cell + embed[pl.ds(ids[row, c], 1), :]))
            for part in range(2):
                start = part * (TOKENS // 2) + (strip * 2 + col // 6) * HALF
                start = pl.multiple_of(start + (inner * 6 + col % 6) * 4, 8)
                rows = [cell[4 * part : 4 * part + 4] for cell in cells]
                put_rows(x, start, jnp.concatenate(rows, axis=0))
        return carry

    lax.fori_loop(0, ROWS, embed_row, 0)

    def pass_on(block):
        wait_opposite(block)
        for i in range(3):
            passed_copy(block, i).start()

    pass_on(0)
    loads[1].wait()
    to_lines(qkv, qkv_lines)
    prepare_weights(qkv_lines, wide, w_q, w_kt, w_v)
    loads[3].wait()
    to_lines(flat_proj, proj_lines)
    for block in range(2):
        w_proj[block] = to_matrix(proj_lines, wide, block, C, C)
    near_part(0)
    pick_and_send(1)
    far_part(0)
    loads[5].wait()
    to_lines(flat_down, down_lines)
    for block in range(2):
        w_down[block] = to_matrix(down_lines, wide, block, 4 * C, C)
    loads[2].wait()
    loads[4].wait()

    def halo(index, source, target, i, j):
        return pltpu.make_async_remote_copy(
            src_ref=source,
            dst_ref=target,
            send_sem=halo_send.at[index],
            recv_sem=halo_recv.at[index],
            device_id=place(i, j),
            device_id_type=pl.DeviceIdType.MESH,
        )

    sent, back = moved.at[0], moved.at[1]
    ahead = [
        halo(0, sent.at[:, 0, 0], received.at[:, 4], north, west),
        halo(1, sent.at[:, 1, 0], received.at[:, 3], north, lon),
        halo(2, sent.at[:, 0, 1], received.at[:, 0], lat, west),
    ]
    ahead += [halo(3 + p, sent.at[p, 0, 3], received.at[p, 2], lat, west) for p in range(2)]
    ahead += [halo(5 + p, sent.at[p, 0, 2], received.at[p, 1], lat, west) for p in range(2)]
    home = []
    for p in range(2):
        home += [
            halo(7 + 3 * p, back.at[p, 1, 3], returned.at[p, 4], south, east),
            halo(8 + 3 * p, back.at[p, 0, 3], returned.at[p, 3], south, lon),
            halo(9 + 3 * p, back.at[p, 1, 2], returned.at[p, 2], lat, east),
        ]
    home += [halo(13 + p, back.at[p, 1, 0:2], returned.at[p, 0:2], lat, east) for p in range(2)]

    def piece(p, strip, half):
        return p * (TOKENS // 2) + (strip * 2 + half) * HALF

    def narrow(block, p, lat_window):
        blank = jnp.zeros((80 - HALF, C), jnp.float32)
        for bh in range(2):
            for half in range(2):
                strip = 2 * lat_window + bh
                rows = take_rows(y, pl.multiple_of(piece(p, strip, half), 8), HALF)
                rows = jnp.concatenate([rows, blank], axis=0)
                moved[block, p, half, strip] = rows.astype(jnp.bfloat16)

    def widen(target, p, strip, half, source):
        put_rows(target, piece(p, strip, half), source.astype(jnp.float32)[:HALF])

    def step(at, carry):
        block = at // 2
        lat_window = jnp.where(block == 0, at, 3 - at)

        @pl.when(lax.rem(at, 2) == 0)
        def _():
            wait_sibling(block)
            spread_tables(block, gathered, spread, tables)

        @pl.when(at == 2)
        def _():
            for p in range(2):
                widen(x, p, 2, 0, sent[p, 1, 3])
            for i in (0, 1, 3, 4):
                ahead[i].wait_recv()
            for p in range(2):
                widen(x, p, 2, 1, received[p, 2])
                widen(x, p, 3, 0, received[p, 3])
                widen(x, p, 3, 1, received[p, 4])

        @pl.when(at == 3)
        def _():
            for p in range(2):
                widen(x, p, 0, 0, sent[p, 1, 1])
                widen(x, p, 1, 0, sent[p, 1, 2])
            for i in (2, 5, 6):
                ahead[i].wait_recv()
            for p in range(2):
                widen(x, p, 0, 1, received[p, 0])
                widen(x, p, 1, 1, received[p, 1])

        @pl.when(at == 0)
        def _():
            pass_on(1)

        run_windows(block, lat_window, lax.rem(at, 1), x, y, tables, consts, weights, lat)

        for p in range(2):
            narrow(block, p, lat_window)

        def after(when, copies):
            @pl.when(at == when)
            def _():
                for copy in copies:
                    copy.start()

        after(0, ahead[0:3])
        after(1, ahead[3:7])
        after(2, home[0:6])
        after(3, home[6:8])

        @pl.when(at == 0)
        def _():
            near_part(1)
            far_part(1)

        return carry

    lax.fori_loop(0, 4, step, 0)

    def gather_levels(p, from_strip, from_half, strip, half):
        for near in range(4):
            level = (4 * p + near + 1) % Z
            for tile in range(2):
                rows = y[tile, pl.ds(piece(p, from_strip, from_half) + near, 18, stride=4), :]
                x[tile, pl.ds((strip * 2 + half) * CELL + level, 18, stride=8), :] = rows

    def put(strip, half):
        def put_row(inner, carry):
            for col in range(6):
                at = pl.multiple_of((strip * 2 + half) * CELL + (inner * 6 + col) * 8, 8)
                lane = (half * 6 + col) * C
                out[strip * 3 + inner, :, lane : lane + C] = take_rows(x, at, 8).astype(jnp.bfloat16)
            return carry

        lax.fori_loop(0, 3, put_row, 0)

    def take_home(i, slot, strip, half):
        for p in range(2):
            widen(y, p, *slot, returned[p, i])
            gather_levels(p, *slot, strip, half)

    for strip in range(3):
        for p in range(2):
            gather_levels(p, strip, 0, strip + 1, 1)
        put(strip + 1, 1)
    for copy in ahead:
        copy.wait_send()
    for block in range(2):
        for i in range(4):
            own_copy(block, i).wait_send()
        for i in range(3):
            passed_copy(block, i).wait_send()
        for part in range(2):
            sibling_copy(block, part).wait_send()
    for copy in home[:6]:
        copy.wait()
    take_home(2, (2, 1), 3, 0)
    take_home(3, (3, 0), 0, 1)
    take_home(4, (3, 1), 0, 0)
    for where in ((3, 0), (0, 1), (0, 0)):
        put(*where)
    for copy in home[6:]:
        copy.wait()
    for strip in range(2):
        take_home(strip, (strip, 1), strip + 1, 0)
        put(strip + 1, 0)


def body(
    tokens,
    surface_ids,
    surface_embed,
    type_index,
    bias_plain,
    bias_shift,
    w_qkv,
    w_proj,
    w_up,
    w_down,
):
    spread = jnp.asarray(spread_matrix(), jnp.bfloat16)
    tail = jnp.asarray(query_tail(), jnp.float32)
    masks = jnp.asarray(mask_rows(), jnp.float32)
    lanes = jnp.asarray(head_lanes(), jnp.float32)
    in_vmem = pl.BlockSpec(memory_space=pltpu.VMEM)
    in_smem = pl.BlockSpec(memory_space=pltpu.SMEM)
    anywhere = pl.BlockSpec(memory_space=pl.ANY)
    rows = pl.pallas_call(
        kernel,
        out_shape=jax.ShapeDtypeStruct((ROWS, Z, COLS * C), jnp.bfloat16),
        in_specs=[anywhere, in_smem, in_smem]
        + [in_vmem] * 3
        + [anywhere]
        + [in_vmem] * 4
        + [anywhere] * 4,
        out_specs=in_vmem,
        scratch_shapes=[
            pltpu.VMEM((ROWS, Z, COLS * C), jnp.bfloat16),
            pltpu.VMEM((8, C), jnp.float32),
            pltpu.VMEM((2, 1104, 128), jnp.float32),
            pltpu.VMEM((4, 128, 384), jnp.bfloat16),
            pltpu.VMEM((3, 64, 128), jnp.float32),
            pltpu.VMEM((2, 48, 384), jnp.bfloat16),
            pltpu.VMEM((2, 6, 256, 256), jnp.bfloat16),
            pltpu.VMEM((2, 3 * C * C), jnp.bfloat16),
            pltpu.VMEM((2, C, HEADS * 128), jnp.bfloat16),
            pltpu.VMEM((2, C, C), jnp.bfloat16),
            pltpu.VMEM((2, C, 256), jnp.bfloat16),
            pltpu.VMEM((2, C, C), jnp.bfloat16),
            pltpu.VMEM((2, C, 4 * C), jnp.bfloat16),
            pltpu.VMEM((2, 4 * C, C), jnp.bfloat16),
            pltpu.VMEM((2, C * C), jnp.bfloat16),
            pltpu.VMEM((2, 4 * C * C), jnp.bfloat16),
            pltpu.VMEM((2, 3 * C * C // 128, 128), jnp.float32),
            pltpu.VMEM((2, C * C // 128, 128), jnp.float32),
            pltpu.VMEM((2, 4 * C * C // 128, 128), jnp.float32),
            pltpu.VMEM((5, 4 * C, 128), jnp.float32),
            pltpu.VMEM((2, 2, 4, 2, 48, 384), jnp.bfloat16),
            pltpu.VMEM((TABLES, WW, 16, 256), jnp.bfloat16),
            pltpu.VMEM((2, TOKENS, 128), jnp.float32),
            pltpu.VMEM((2, TOKENS, 128), jnp.float32),
            pltpu.VMEM((2, 2, 2, STRIPS, 80, C), jnp.bfloat16),
            pltpu.VMEM((2, 5, 80, C), jnp.bfloat16),
            pltpu.VMEM((2, 5, 80, C), jnp.bfloat16),
            pltpu.SemaphoreType.DMA((6,)),
            pltpu.SemaphoreType.DMA((2, 9)),
            pltpu.SemaphoreType.DMA((2, 9)),
            pltpu.SemaphoreType.DMA((15,)),
            pltpu.SemaphoreType.DMA((15,)),
        ],
        compiler_params=pltpu.CompilerParams(
            collective_id=0, has_side_effects=True, vmem_limit_bytes=56 * 1024 * 1024
        ),
    )(
        tokens.transpose(1, 0, 2),
        surface_ids,
        type_index,
        surface_embed,
        bias_plain.reshape(SHARD_LINES, 128),
        bias_shift.reshape(SHARD_LINES, 128),
        spread,
        tail,
        masks,
        lanes,
        jnp.asarray(head_spread(), jnp.bfloat16),
        w_qkv,
        w_proj,
        w_up,
        w_down,
    )
    return rows.transpose(1, 0, 2)


def solution(mesh):
    return jax.shard_map(
        body,
        mesh=mesh,
        in_specs=(
            P(None, "lat", "lon"),
            P("lat", "lon"),
            P(),
            P("lat"),
            P("lon"),
            P("lon"),
            P(),
            P(),
            P(),
            P(),
        ),
        out_specs=P(None, "lat", "lon"),
        check_vma=False,
    )
```
